256 devices in a mesh: context: 32 (over x, z), mp: 8 (over y, core).
Axes of the slice: x: 4, y: 4, z: 8, core: 2. Of those that a mesh axis runs over, the one named last changes fastest.
Arguments:
- queries: bfloat16 [4096, 8192], P('context', 'mp'), may hold values from -12 to 12
- query_pos: int32 [4096], P('context'), may hold values from 0 to 131071, as said below
- k_cache: bfloat16 [131072, 1024], P('context', 'mp'), may hold values from -6 to 6
- v_cache: bfloat16 [131072, 1024], P('context', 'mp'), may hold values from -6 to 6
- kept_index: int32 [16384], P('context'), may hold values from 0 to 4095, as said below
- kept_count: int32 [32], P('context'), may hold values from 1 to 512, as said below
- route: int32 [4096], P('context'), may hold values from 0 to 4095, as said below
Outputs:
- balanced_out: bfloat16 [4096, 8192], P('context', 'mp')
The draws below stay inside these ranges and needn't reach their ends.
Inputs may be any that keep to these rules, and one draw needn't show every extreme that they name: `query_pos`: each context index's 128 entries lie in its own block of 4096 positions, distinct and ascending. `kept_index`: each context index's 512 entries are local positions in its block; the live ones come first, distinct and ascending, and the rest are 0. The list of context index 0 starts with position 0. `kept_count`: some context index has all 512 slots live. `route`: A permutation of the 4096 rows; the rows of one context index go in equal shares to the blocks of 128 output rows of all context indices.
All inputs are finite; a program needn't handle non-finite values.
Results may differ from the reference program's by a relative error of at most 0.018.
Values may be sent and summed in bfloat16 or wider, within the bound.
A program may use at most 128 MiB of HBM per device.

```python
import math
import jax
import jax.numpy as jnp
from jax import lax

H = 64
KVH = 8
HD = 128
LOC = 4096
KCAP = 512
Q_DEV = 128
PROMPT = 131072
KEPT = 16384
QTOT = 4096


def kept_totals(key):
    key = jax.random.fold_in(key, 5)
    first_key, second_key = jax.random.split(key)
    device_count = KEPT // KCAP
    totals = jax.random.randint(first_key, (device_count,), 1, KCAP + 1)
    full_device = jax.random.randint(second_key, (), 0, device_count)
    return jnp.where(jnp.arange(device_count) == full_device, KCAP, totals).astype(jnp.int32)


def draw_queries(key, part):
    key = jax.random.fold_in(key, 11)
    first_key = jax.random.fold_in(key, 0)
    values = jnp.clip(2.5 * jax.random.normal(first_key, (QTOT, H * HD), jnp.float32), -12.0, 12.0)
    return values.astype(jnp.bfloat16)


def draw_k_cache(key, part):
    key = jax.random.fold_in(key, 17)
    first_key = jax.random.fold_in(key, 0)
    values = jnp.clip(jax.random.normal(first_key, (PROMPT, KVH * HD), jnp.float32), -6.0, 6.0)
    return values.astype(jnp.bfloat16)


def draw_kept_count(key, part):
    return kept_totals(key)


def draw_kept_index(key, part):
    totals = kept_totals(key)
    key = jax.random.fold_in(key, 7)
    device_count = KEPT // KCAP
    device_keys = jax.random.split(key, device_count)
    kept_lists = jax.vmap(lambda one_key: jnp.sort(jax.random.permutation(one_key, LOC)[:KCAP]))(device_keys)
    kept_lists = kept_lists.at[0, 0].set(0)
    slot_ids = jnp.arange(KCAP)[None, :]
    kept_lists = jnp.where(slot_ids < totals[:, None], kept_lists, 0)
    return kept_lists.reshape(KEPT).astype(jnp.int32)


def draw_query_pos(key, part):
    key = jax.random.fold_in(key, 23)
    device_count = QTOT // Q_DEV
    device_keys = jax.random.split(key, device_count)
    local_lists = jax.vmap(lambda one_key: jnp.sort(jax.random.permutation(one_key, LOC)[:Q_DEV]))(device_keys)
    offsets = (jnp.arange(device_count) * LOC)[:, None]
    return (local_lists + offsets).reshape(QTOT).astype(jnp.int32)


def draw_route(key, part):
    key = jax.random.fold_in(key, 13)
    device_count = QTOT // Q_DEV
    per_device = Q_DEV // device_count
    first_key, second_key = jax.random.split(key)
    send_order = jax.vmap(lambda one_key: jax.random.permutation(one_key, Q_DEV))(jax.random.split(first_key, device_count))
    slot_perm = jax.vmap(lambda one_key: jax.random.permutation(one_key, Q_DEV))(jax.random.split(second_key, device_count))
    destination = send_order // per_device
    source = jnp.arange(device_count)[:, None]
    slot_in_block = source * per_device + send_order % per_device
    target = destination * Q_DEV + slot_perm[destination, slot_in_block]
    return target.reshape(QTOT).astype(jnp.int32)


def level_of(key, shape, pieces, low, top_value):
    gain = 1.0
    for position, parts in pieces:
        heights = jax.random.uniform(jax.random.fold_in(jax.random.fold_in(key, 6), position), (parts,), jnp.float32, low / len(pieces), top_value / len(pieces))
        gain = gain * jnp.repeat(jnp.exp(heights), shape[position] // parts).reshape((-1,) + (1,) * (len(shape) - 1 - position))
    return gain


def bell_draw(own_key, dims, deviation, reach, pieces=(), kind=jnp.bfloat16):
    result = jax.random.normal(own_key, dims, jnp.float32) * deviation
    if len(pieces) > 0:
        result = level_of(own_key, dims, pieces, -0.22, 0.18) * result
    return jnp.clip(result, min=-reach, max=reach).astype(kind)


def setup_inputs(seed: int = 0) -> dict:
    seeds = jax.random.split(jax.random.key(seed), 8)
    return {
        "queries": draw_queries(jax.random.fold_in(seeds[7], 71), 0),
        "query_pos": draw_query_pos(jax.random.fold_in(seeds[7], 71), 0),
        "k_cache": draw_k_cache(jax.random.fold_in(seeds[7], 71), 0),
        "v_cache": bell_draw(seeds[3], (PROMPT, KVH * HD), 1.0, 6.0, ((0, 32), (1, 8))),
        "kept_index": draw_kept_index(jax.random.fold_in(seeds[7], 71), 0),
        "kept_count": draw_kept_count(jax.random.fold_in(seeds[7], 71), 0),
        "route": draw_route(jax.random.fold_in(seeds[7], 71), 0),
    }


far_away = 2 ** 30
neg_large = -1e+30

def reference(queries, query_pos, k_cache, v_cache, kept_index, kept_count, route):
    slot_ids = jnp.arange(KEPT, dtype=jnp.int32)
    owner_device = slot_ids // KCAP
    prompt_rows = (kept_index + owner_device * LOC).astype(jnp.int32)
    is_live = slot_ids % KCAP < kept_count[owner_device]
    key_pos = jnp.where(is_live, prompt_rows, far_away).astype(jnp.int32)
    kept_keys = k_cache[prompt_rows].astype(jnp.float32).reshape(KEPT, KVH, HD)
    kept_vals = v_cache[prompt_rows].astype(jnp.float32).reshape(KEPT, KVH, HD)
    group_size = H // KVH
    block_rows = 32
    scale = 1.0 / math.sqrt(HD)

    def score_block(operands):
        query_block, pos_block = operands
        query_heads = query_block.astype(jnp.float32).reshape(block_rows, KVH, group_size, HD)
        scores = jnp.einsum('qhgd,khd->qhgk', query_heads, kept_keys) * scale
        visible = key_pos[None, None, None, :] <= pos_block[:, None, None, None]
        scores = jnp.where(visible, scores, neg_large)
        row_peak = lax.optimization_barrier(jnp.max(scores, axis=-1, keepdims=True))
        weights = jnp.where(visible, jnp.exp(scores - row_peak), 0.0)
        denominator = lax.optimization_barrier(jnp.sum(weights, axis=-1))
        weights_bf = lax.optimization_barrier(weights.astype(jnp.bfloat16)).astype(jnp.float32)
        numerator = jnp.einsum('qhgk,khd->qhgd', weights_bf, kept_vals)
        return (numerator / denominator[..., None]).astype(jnp.bfloat16).reshape(block_rows, H * HD)
    attended = lax.map(score_block, (queries.reshape(QTOT // block_rows, block_rows, H * HD), query_pos.reshape(QTOT // block_rows, block_rows)))
    attended = attended.reshape(QTOT, H * HD)
    return jnp.zeros_like(attended).at[route].set(attended)
```

```python
import math

import jax
import jax.numpy as jnp
from jax import lax
from jax.experimental import pallas as pl
from jax.experimental.pallas import tpu as pltpu
from jax.sharding import PartitionSpec as P

MESH = pl.DeviceIdType.MESH
F32, BF16, I32 = jnp.float32, jnp.bfloat16, jnp.int32

HD = 128
NX = 4
NZ = 8
ROWS = 128
HEADS = 8
SLOTS = 512
HALF = SLOTS // 2
LOCAL = 4096
QROWS = ROWS * HEADS
CHUNK = QROWS // NX
TILES = 8
FAR = 1 << 29
LOW = -1e30
HIDDEN = -2e30
QSCALE = math.log2(math.e) / math.sqrt(HD)


def iota(shape, axis):
    return lax.broadcasted_iota(I32, shape, axis)


def kernel(
    meta_ref, q_ref, k_ref, v_ref, out_ref,
    cache, spare, ring, kk, vv, kkd, vvd, qraw, qp, acc, peak, part, partl, got, gotl, fin, gath,
    table, slots, ohf,
    load_sem, swap_s, swap_r, ring_s, ring_r, q_s, q_r, ret_s, ret_r, retl_s, retl_r,
    a2a_s, a2a_r, tx_s, tx_r, tz_s, tz_r,
):
    c = lax.axis_index("context")
    x = lax.div(c, NZ)
    z = lax.rem(c, NZ)
    mirror = NX - 1 - x

    def at(xx, zz):
        return {"context": xx * NZ + zz}

    def xplus(n):
        return lax.rem(x + n, NX)

    def zplus(n):
        return lax.rem(z + n, NZ)

    def remote(src, dst, send, recv, to):
        return pltpu.make_async_remote_copy(
            src_ref=src, dst_ref=dst, send_sem=send, recv_sem=recv, device_id=to, device_id_type=MESH
        )

    barrier = pltpu.get_barrier_semaphore()
    for n in range(1, NX):
        pl.semaphore_signal(barrier, inc=1, device_id=at(xplus(n), z), device_id_type=MESH)
    for n in range(1, NZ):
        pl.semaphore_signal(barrier, inc=1, device_id=at(x, zplus(n)), device_id_type=MESH)

    loads = []
    for i in range(4):
        rows = pl.ds(i * 1024, 1024)
        for side, ref in enumerate((k_ref, v_ref)):
            copy = pltpu.make_async_copy(
                ref.at[rows], cache.at[rows, pl.ds(side * HD, HD)], load_sem.at[i, side]
            )
            copy.start()
            loads.append(copy)

    meta = meta_ref[...]
    qpos_lane = meta[0:1]
    route_lane = meta[1:2]
    count = meta[6:7]
    eye = iota((128, 128), 0) == iota((128, 128), 1)

    def column(row):
        return jnp.sum(jnp.where(eye, row.astype(F32), 0.0), axis=1, keepdims=True).astype(I32)

    def gather(half):
        index = jnp.concatenate([column(meta[2 + 2 * half:3 + 2 * half]), column(meta[3 + 2 * half:4 + 2 * half])], 0)
        total = jnp.zeros((HALF, 2 * HD), F32)
        for i in range(4):
            if half == 1:
                loads[2 * i].wait()
                loads[2 * i + 1].wait()
            hit = iota((HALF, 1024), 1) == index - 1024 * i
            one = jnp.where(hit, 1.0, 0.0).astype(BF16)
            total += jnp.dot(one, cache[pl.ds(i * 1024, 1024), :], preferred_element_type=F32)
        live = iota((HALF, HD), 0) + HALF * half < count
        return jnp.concatenate([total[:, :HD], jnp.where(live, total[:, HD:], 0.0)], 1).astype(BF16)

    spare[...] = gather(1)
    pl.semaphore_wait(barrier, NX - 1 + NZ - 1)
    swap = remote(spare, ring.at[0, 1], swap_s, swap_r, at(mirror, z))
    swap.start()
    ring[0, 0] = gather(0)
    right, left = at(x, zplus(1)), at(x, zplus(NZ - 1))

    def pass_right(source, target):
        return remote(ring.at[source, 0], ring.at[target, 0], ring_s.at[target, 0], ring_r.at[target, 0], right)

    def pass_left(source, target):
        return remote(ring.at[source, 1], ring.at[target, 1], ring_s.at[target, 1], ring_r.at[target, 1], left)

    def own_pass(half, target):
        return (
            remote(ring.at[0, half], ring.at[target, 0], ring_s.at[target, 0], ring_r.at[target, 0], right),
            remote(ring.at[0, half], ring.at[target, 1], ring_s.at[target, 1], ring_r.at[target, 1], left),
        )

    for copy in own_pass(0, 1):
        copy.start()

    dest_lane = lax.div(route_lane, ROWS)
    dest_col = column(dest_lane)
    same = dest_col == dest_lane
    first = iota((128, 128), 0)
    second = iota((128, 128), 1)
    before_lane = jnp.sum(jnp.where(same & (first < second), 1.0, 0.0), axis=0, keepdims=True).astype(I32)
    before_col = jnp.sum(jnp.where(same & (second < first), 1.0, 0.0), axis=1, keepdims=True).astype(I32)
    rank_lane = dest_lane * (ROWS // (NX * NZ)) + before_lane
    rank_col = dest_col * (ROWS // (NX * NZ)) + before_col
    slot_col = column(lax.rem(route_lane, ROWS)).astype(F32)
    slot_row = jnp.sum(jnp.where(rank_col == second, slot_col, 0.0), axis=0, keepdims=True).astype(I32)
    table[z, x] = slot_row + ROWS * count

    def table_x(n):
        return remote(table.at[z, x], table.at[z, x], tx_s.at[n], tx_r.at[n], at(xplus(n), z))

    for n in range(1, NX):
        table_x(n).start()

    stacked = jnp.concatenate([q_ref[:, h * HD:(h + 1) * HD] for h in range(HEADS)], 0)
    rank_key = jnp.concatenate([rank_lane + ROWS * h for h in range(HEADS)], 1)
    within = iota((CHUNK, 1), 0)
    place = lax.div(within, 32) * 4 + lax.rem(within, 4)
    head_of = lax.rem(lax.div(within, 4), HEADS)
    for i in range(NX):
        hit = rank_key == place + 32 * i + ROWS * head_of
        one = jnp.where(hit, 1.0, 0.0).astype(BF16)
        qraw[x, i] = jnp.dot(one, stacked, preferred_element_type=F32).astype(BF16)

    q_right, q_left = at(xplus(1), z), at(xplus(NX - 1), z)

    def q_send(owner, half, number, to):
        view = qraw.at[owner, pl.ds(2 * half, 2)]
        return remote(view, view, q_s.at[number], q_r.at[number], to)

    q_copies = [
        q_send(x, 0, 0, q_right), q_send(x, 1, 3, q_left),
        q_send(x, 1, 1, q_right), q_send(x, 0, 2, q_left),
    ]
    for copy in q_copies:
        copy.start()

    def split_queries(owner):
        for i in range(NX):
            scaled = qraw[owner, i].astype(F32) * QSCALE
            high = scaled.astype(BF16)
            low = (scaled - high.astype(F32)).astype(BF16)
            qp[owner, i] = jnp.concatenate([high, low], 1)

    split_queries(x)
    for n in range(1, NX):
        acc[xplus(n)] = jnp.zeros((NX, CHUNK, 2 * HD), F32)
        peak[xplus(n)] = jnp.full((NX, CHUNK, HD), LOW, F32)

    def keys_of(block):
        keys = jnp.transpose(block[:, :HD])
        return jnp.concatenate([keys, keys], 0)

    def values_of(block, live):
        return jnp.concatenate([block[:, HD:], jnp.where(live, 1.0, 0.0).astype(BF16)], 1)

    whole = jnp.concatenate([ring[0, 0], spare[...]], 0)
    kkd[...] = keys_of(whole)
    vvd[...] = values_of(whole, iota((SLOTS, HD), 0) < count)
    lane = iota((1, SLOTS), 1)
    count_wide = jnp.concatenate([count] * 4, 1)
    key_pos = jnp.where(lane < count_wide, jnp.concatenate([meta[i:i + 1] for i in range(2, 6)], 1), FAR)
    for i in range(NX):
        own_pos = jnp.sum(
            jnp.where(rank_lane == place + 32 * i, qpos_lane.astype(F32), 0.0), axis=1, keepdims=True
        ).astype(I32)
        scores = jnp.dot(qp[x, i], kkd[...], preferred_element_type=F32)
        scores = jnp.where(key_pos <= own_pos, scores, HIDDEN)
        new_peak = jnp.maximum(jnp.max(scores, axis=1, keepdims=True), LOW)
        weights = jnp.exp2(scores - new_peak).astype(BF16)
        acc[x, i] = jnp.dot(weights, vvd[...], preferred_element_type=F32)
        peak[x, i] = jnp.broadcast_to(new_peak, (CHUNK, HD))

    swap.wait_recv()
    for copy in own_pass(1, 2):
        copy.start()

    for n in range(1, NX):
        table_x(n).wait_recv()

    def table_z(n):
        return remote(table.at[z], table.at[z], tz_s.at[n], tz_r.at[n], at(x, zplus(n)))

    for n in range(1, NZ):
        table_z(n).start()

    def halves_of(t):
        step = lax.div(t + 1, 2)
        odd = lax.rem(t, 2) == 1
        ends = (t == 0) | (t == TILES - 1)
        group0 = jnp.where(ends | odd, x, mirror)
        group1 = jnp.where(ends | (~odd), mirror, x)
        shift0 = jnp.where(ends | odd, 0, HALF)
        shift1 = jnp.where(ends | (~odd), HALF, 0)
        return (group0, lax.rem(z - step + NZ, NZ), shift0), (group1, lax.rem(z + step, NZ), shift1)

    def prepare(t):
        block = ring[t].reshape(SLOTS, 2 * HD)
        kk[t] = keys_of(block)
        lives = []
        for group, origin, shift in halves_of(t):
            live_count = lax.div(table[origin, group], ROWS)
            lives.append(iota((HALF, HD), 0) + shift < live_count)
        vv[t] = values_of(block, jnp.concatenate(lives, 0))

    prepare(0)

    def seen(owner, half):
        group, origin, shift = half
        return (owner > group) | ((owner == group) & (origin < z))

    def attend(t, owner):
        half0, half1 = halves_of(t)
        seen0, seen1 = seen(owner, half0), seen(owner, half1)

        @pl.when(seen0 | seen1)
        def _():
            bias0 = jnp.where(seen0, 0.0, HIDDEN)
            bias1 = jnp.where(seen1, 0.0, HIDDEN)
            bias = jnp.where(lane < HALF, bias0, bias1)
            for i in range(NX):
                scores = jnp.dot(qp[owner, i], kk[t], preferred_element_type=F32) + bias
                old_peak = peak[owner, i]
                new_peak = jnp.maximum(jnp.max(scores, axis=1, keepdims=True), old_peak)
                weights = jnp.exp2(scores - new_peak[:, :1]).astype(BF16)
                scale = jnp.exp2(old_peak - new_peak)
                summed = jnp.dot(weights, vv[t], preferred_element_type=F32)
                acc[owner, i] = acc[owner, i] * jnp.concatenate([scale, scale], 1) + summed
                peak[owner, i] = new_peak

    def takes_part(source, owner):
        return jnp.minimum(source, NX - 1 - source) <= owner

    def ret(n, owner):
        xd = xplus(n)
        return (
            remote(part.at[owner, xd], got.at[x, owner], ret_s.at[n, owner], ret_r.at[n, owner], at(xd, z)),
            remote(partl.at[xd, owner], gotl.at[x, owner], retl_s.at[n, owner], retl_r.at[n, owner], at(xd, z)),
        )

    def finish(owner):
        for i in range(NX):
            top = acc[owner, i][:, :HD]
            bottom = acc[owner, i][:, HD:]
            alive = bottom > 0.0
            safe = jnp.where(alive, bottom, 1.0)
            part[owner, i] = (top / safe).astype(BF16)
            logs = jnp.where(alive, peak[owner, i] + jnp.log(safe) * math.log2(math.e), LOW)
            for j in range(2):
                partl[i, owner, j] = jnp.sum(
                    jnp.where(eye, logs[j * 128:(j + 1) * 128], 0.0), axis=0, keepdims=True
                )

        @pl.when(takes_part(x, owner))
        def _():
            for n in range(1, NX):
                for copy in ret(n, owner):
                    copy.start()

        got[x, owner] = part[owner, x]
        gotl[x, owner] = partl[x, owner]

    def one_step(t, carry):
        pass_right(t, t).wait_recv()
        pass_left(t, t).wait_recv()

        @pl.when(t <= 5)
        def _():
            pass_right(t, t + 2).start()

        @pl.when((t <= 4) | (t == 6))
        def _():
            pass_left(t, jnp.minimum(t + 2, TILES - 1)).start()

        @pl.when(t == 1)
        def _():
            q_send(xplus(NX - 1), 0, 0, q_right).wait_recv()
            q_send(xplus(NX - 1), 0, 4, q_right).start()
            q_send(xplus(1), 1, 3, q_left).wait_recv()
            q_send(xplus(1), 1, 5, q_left).start()
            for n in range(1, NZ):
                table_z(n).wait_recv()

        @pl.when(t == 2)
        def _():
            q_send(xplus(NX - 1), 1, 1, q_right).wait_recv()
            q_send(xplus(1), 0, 2, q_left).wait_recv()
            split_queries(xplus(1))
            split_queries(xplus(NX - 1))

        @pl.when(t == 3)
        def _():
            q_send(xplus(2), 0, 4, q_right).wait_recv()
            q_send(xplus(2), 1, 5, q_left).wait_recv()
            split_queries(xplus(2))

        prepare(t)

        def one_owner(n, inner):
            owner = xplus(n)
            ready = jnp.where(n == 0, 1, jnp.where(n == 2, 3, 2))
            lowest = jnp.where(t < ready, t + 1, jnp.where(t == ready, 0, t))

            def one_tile(u, innermost):
                attend(u, owner)
                return innermost

            lax.fori_loop(lowest, t + 1, one_tile, 0)

            @pl.when(t == TILES - 1)
            def _():
                finish(owner)

            return inner

        lax.fori_loop(0, NX, one_owner, 0)
        return carry

    lax.fori_loop(1, TILES, one_step, 0)

    def rows_of(row):
        return jnp.sum(jnp.where(eye, row, 0.0), axis=1, keepdims=True)

    for owner in range(NX):
        sources = [s for s in range(NX) if min(s, NX - 1 - s) <= owner]
        for n in range(1, NX):
            @pl.when(takes_part(xplus(NX - n), owner))
            def _():
                for copy in ret(n, owner):
                    copy.wait_recv()
        logs = [
            jnp.concatenate([rows_of(gotl[s, owner, j]) for j in range(2)], 0) for s in sources
        ]
        most = logs[0]
        for value in logs[1:]:
            most = jnp.maximum(most, value)
        total = jnp.zeros((CHUNK, HD), F32)
        weight = jnp.zeros((CHUNK, 1), F32)
        for s, value in zip(sources, logs):
            share = jnp.exp2(value - most)
            weight = weight + share
            total = total + share * got[s, owner].astype(F32)
        fin[owner] = (total / weight).astype(BF16).reshape(NZ, CHUNK // NZ, HD)

    def spread(n):
        zd = zplus(n)
        return remote(fin.at[:, zd], gath.at[z], a2a_s.at[n], a2a_r.at[n], at(x, zd))

    for n in range(1, NZ):
        spread(n).start()
    gath[z] = fin[:, z]

    for zz in range(NZ):
        for xx in range(NX):
            slots[zz * NX + xx:zz * NX + xx + 1, :] = lax.rem(table[zz, xx], ROWS).astype(F32)
    wide = iota((128, QROWS), 1)
    pick = jnp.where(iota((128, QROWS), 0) == c * 4 + lax.rem(wide, 4), 1.0, 0.0).astype(BF16)
    picked = jnp.dot(slots[...].astype(BF16), pick, preferred_element_type=F32)
    mine = iota((32, QROWS), 0) == lax.div(iota((32, QROWS), 1), 32)
    slot_of = jnp.sum(jnp.where(mine, picked, 0.0), axis=0, keepdims=True).astype(I32)
    lanes = iota((1, QROWS), 1)
    key = slot_of + ROWS * lax.rem(lax.div(lanes, 4), HEADS)
    for h in range(HEADS):
        hit = iota((ROWS, QROWS), 0) + ROWS * h == key
        ohf[h] = jnp.where(hit, 1.0, 0.0).astype(BF16)

    for n in range(1, NZ):
        spread(n).wait_recv()
    arrived = gath[...].reshape(QROWS, HD)
    for h in range(HEADS):
        out_ref[:, h * HD:(h + 1) * HD] = jnp.dot(
            ohf[h], arrived, preferred_element_type=F32
        ).astype(BF16)

    swap.wait_send()
    for copy in own_pass(0, 1) + own_pass(1, 2):
        copy.wait_send()
    for t in range(1, 6):
        pass_right(t, t + 2).wait_send()
    for t in (1, 2, 3, 4, 6):
        pass_left(t, min(t + 2, TILES - 1)).wait_send()
    for copy in q_copies:
        copy.wait_send()
    q_send(xplus(NX - 1), 0, 4, q_right).wait_send()
    q_send(xplus(1), 1, 5, q_left).wait_send()
    for n in range(1, NX):
        table_x(n).wait_send()
        for owner in range(NX):
            @pl.when(takes_part(x, owner))
            def _():
                for copy in ret(n, owner):
                    copy.wait_send()
    for n in range(1, NZ):
        table_z(n).wait_send()
        spread(n).wait_send()


def per_device(queries, query_pos, k_cache, v_cache, kept_index, kept_count, route):
    device_index = lax.axis_index("context")
    live = jnp.arange(SLOTS, dtype=I32) < kept_count[0]
    index = jnp.where(live, kept_index, kept_index[0])
    meta = jnp.concatenate(
        [
            (query_pos - device_index * LOCAL)[None],
            route[None],
            index.reshape(4, 128),
            jnp.broadcast_to(kept_count[0], (2, 128)),
        ],
        0,
    )
    dma = pltpu.SemaphoreType.DMA
    vmem = pltpu.VMEM
    return pl.pallas_call(
        kernel,
        out_shape=jax.ShapeDtypeStruct((ROWS, QROWS), BF16),
        in_specs=[
            pl.BlockSpec(memory_space=vmem),
            pl.BlockSpec(memory_space=vmem),
            pl.BlockSpec(memory_space=pl.ANY),
            pl.BlockSpec(memory_space=pl.ANY),
        ],
        out_specs=pl.BlockSpec(memory_space=vmem),
        scratch_shapes=[
            vmem((LOCAL, 2 * HD), BF16),
            vmem((HALF, 2 * HD), BF16),
            vmem((TILES, 2, HALF, 2 * HD), BF16),
            vmem((TILES, 2 * HD, SLOTS), BF16),
            vmem((TILES, SLOTS, 2 * HD), BF16),
            vmem((2 * HD, SLOTS), BF16),
            vmem((SLOTS, 2 * HD), BF16),
            vmem((NX, NX, CHUNK, HD), BF16),
            vmem((NX, NX, CHUNK, 2 * HD), BF16),
            vmem((NX, NX, CHUNK, 2 * HD), F32),
            vmem((NX, NX, CHUNK, HD), F32),
            vmem((NX, NX, CHUNK, HD), BF16),
            vmem((NX, NX, 2, 1, 128), F32),
            vmem((NX, NX, CHUNK, HD), BF16),
            vmem((NX, NX, 2, 1, 128), F32),
            vmem((NX, NZ, CHUNK // NZ, HD), BF16),
            vmem((NZ, NX, CHUNK // NZ, HD), BF16),
            vmem((NZ, NX, 1, 128), I32),
            vmem((NZ * NX, 128), F32),
            vmem((HEADS, ROWS, QROWS), BF16),
            dma((4, 2)), dma, dma,
            dma((TILES, 2)), dma((TILES, 2)),
            dma((6,)), dma((6,)),
            dma((NX, NX)), dma((NX, NX)), dma((NX, NX)), dma((NX, NX)),
            dma((NZ,)), dma((NZ,)),
            dma((NX,)), dma((NX,)),
            dma((NZ,)), dma((NZ,)),
        ],
        compiler_params=pltpu.CompilerParams(
            collective_id=0, has_side_effects=True, vmem_limit_bytes=56 * 1024 * 1024
        ),
    )(meta, queries, k_cache, v_cache)


def solution(mesh):
    placed = (
        P("context", "mp"),
        P("context"),
        P("context", "mp"),
        P("context", "mp"),
        P("context"),
        P("context"),
        P("context"),
    )
    return jax.shard_map(
        per_device, mesh=mesh, in_specs=placed, out_specs=P("context", "mp"), check_vma=False
    )
```

```python
import math

import jax
import jax.numpy as jnp
from jax import lax
from jax.experimental import pallas as pl
from jax.experimental.pallas import tpu as pltpu
from jax.sharding import PartitionSpec as P

MESH = pl.DeviceIdType.MESH
F32, BF16, I32 = jnp.float32, jnp.bfloat16, jnp.int32

HD = 128
NX = 4
NZ = 8
ROWS = 128
HEADS = 8
SLOTS = 512
HALF = SLOTS // 2
LOCAL = 4096
QROWS = ROWS * HEADS
CHUNK = QROWS // NX
TILES = 8
FAR = 1 << 29
LOW = -1e30
HIDDEN = -2e30
QSCALE = math.log2(math.e) / math.sqrt(HD)


def iota(shape, axis):
    return lax.broadcasted_iota(I32, shape, axis)


def kernel(
    idx_hbm, route_hbm, qpos_hbm, q_hbm, k_hbm, v_hbm, count_ref, out_ref,
    cache, hot, idx_ref, route_ref, qpos_ref, q_ref,
    spare, ring, kk, vv, kkd, vvd, qraw, qp, acc, peak, part, partl, got, gotl, fin, gath,
    table, slots, ohf,
    load_sem, small_sem, swap_s, swap_r, ring_s, ring_r, q_s, q_r, ret_s, ret_r, retl_s, retl_r,
    a2a_s, a2a_r, tx_s, tx_r, tz_s, tz_r,
):
    c = lax.axis_index("context")
    x = lax.div(c, NZ)
    z = lax.rem(c, NZ)
    mirror = NX - 1 - x
    right, left = (x, lax.rem(z + 1, NZ)), (x, lax.rem(z + NZ - 1, NZ))

    def at(where):
        return {"context": where[0] * NZ + where[1]}

    def xplus(n):
        return lax.rem(x + n, NX)

    def zplus(n):
        return lax.rem(z + n, NZ)

    def remote(src, dst, send, recv, to):
        return pltpu.make_async_remote_copy(
            src_ref=src, dst_ref=dst, send_sem=send, recv_sem=recv, device_id=at(to), device_id_type=MESH
        )

    smalls = []
    for i, (src, dst) in enumerate(
        ((idx_hbm, idx_ref), (route_hbm, route_ref), (qpos_hbm, qpos_ref), (q_hbm, q_ref))
    ):
        copy = pltpu.make_async_copy(src, dst, small_sem.at[i])
        copy.start()
        smalls.append(copy)
    loads = []
    for i in range(4):
        rows = pl.ds(i * 1024, 1024)
        for side, ref in enumerate((k_hbm, v_hbm)):
            copy = pltpu.make_async_copy(
                ref.at[rows], cache.at[rows, pl.ds(side * HD, HD)], load_sem.at[i, side]
            )
            copy.start()
            loads.append(copy)

    barrier = pltpu.get_barrier_semaphore()
    for n in range(1, NX):
        pl.semaphore_signal(barrier, inc=1, device_id=at((xplus(n), z)), device_id_type=MESH)
    for n in range(1, NZ):
        pl.semaphore_signal(barrier, inc=1, device_id=at((x, zplus(n))), device_id_type=MESH)

    count = count_ref[0]
    eye = iota((128, 128), 0) == iota((128, 128), 1)
    lane = iota((1, 128), 1)

    def column(row):
        return jnp.sum(jnp.where(eye, row.astype(F32), 0.0), axis=1, keepdims=True).astype(I32)

    for copy in smalls[:3]:
        copy.wait()
    kept = idx_ref[...]
    repeat = jnp.broadcast_to(kept[0:1, 0:1], (1, 128))
    for i in (2, 3, 0, 1):
        index = column(jnp.where(lane + 128 * i < count, kept[i:i + 1], repeat))
        for j in range(4):
            hit = iota((128, 1024), 1) == index - 1024 * j
            hot[i * 128:(i + 1) * 128, j * 1024:(j + 1) * 1024] = jnp.where(hit, 1.0, 0.0).astype(BF16)

    route_lane = route_ref[...]
    dest_lane = lax.div(route_lane, ROWS)
    dest_col = column(dest_lane)
    same = dest_col == dest_lane
    first = iota((128, 128), 0)
    second = iota((128, 128), 1)
    before_lane = jnp.sum(jnp.where(same & (first < second), 1.0, 0.0), axis=0, keepdims=True).astype(I32)
    before_col = jnp.sum(jnp.where(same & (second < first), 1.0, 0.0), axis=1, keepdims=True).astype(I32)
    rank_lane = dest_lane * (ROWS // (NX * NZ)) + before_lane
    rank_col = dest_col * (ROWS // (NX * NZ)) + before_col
    slot_col = column(lax.rem(route_lane, ROWS)).astype(F32)
    slot_row = jnp.sum(jnp.where(rank_col == second, slot_col, 0.0), axis=0, keepdims=True).astype(I32)
    table[z, x] = slot_row + ROWS * count

    def gather(half):
        total = jnp.dot(hot[half * HALF:(half + 1) * HALF, :], cache[...], preferred_element_type=F32)
        live = iota((HALF, HD), 0) + HALF * half < count
        keys = jnp.transpose(total[:, :HD].astype(BF16))
        values = jnp.where(live, total[:, HD:], 0.0).astype(BF16)
        return jnp.concatenate([keys, jnp.concatenate([values[:HD], values[HD:]], 1)], 0)

    for copy in loads:
        copy.wait()
    spare[...] = gather(1)
    pl.semaphore_wait(barrier, NX - 1 + NZ - 1)
    swap = remote(spare, ring.at[0, 1], swap_s, swap_r, (mirror, z))
    swap.start()
    ring[0, 0] = gather(0)

    def pass_right(source, target):
        return remote(ring.at[source, 0], ring.at[target, 0], ring_s.at[target, 0], ring_r.at[target, 0], right)

    def pass_left(source, target):
        return remote(ring.at[source, 1], ring.at[target, 1], ring_s.at[target, 1], ring_r.at[target, 1], left)

    def own_pass(half, target):
        return (
            remote(ring.at[0, half], ring.at[target, 0], ring_s.at[target, 0], ring_r.at[target, 0], right),
            remote(ring.at[0, half], ring.at[target, 1], ring_s.at[target, 1], ring_r.at[target, 1], left),
        )

    for copy in own_pass(0, 1):
        copy.start()

    def table_x(n):
        return remote(table.at[z, x], table.at[z, x], tx_s.at[n], tx_r.at[n], (xplus(n), z))

    for n in range(1, NX):
        table_x(n).start()

    smalls[3].wait()
    stacked = jnp.concatenate([q_ref[:, h * HD:(h + 1) * HD] for h in range(HEADS)], 0)
    rank_key = jnp.concatenate([rank_lane + ROWS * h for h in range(HEADS)], 1)
    within = iota((CHUNK, 1), 0)
    place = lax.div(within, 32) * 4 + lax.rem(within, 4)
    head_of = lax.rem(lax.div(within, 4), HEADS)
    for i in range(NX):
        hit = rank_key == place + 32 * i + ROWS * head_of
        one = jnp.where(hit, 1.0, 0.0).astype(BF16)
        qraw[x, i] = jnp.dot(one, stacked, preferred_element_type=F32).astype(BF16)

    q_right, q_left = (xplus(1), z), (xplus(NX - 1), z)

    def q_send(owner, half, number, to):
        view = qraw.at[owner, pl.ds(2 * half, 2)]
        return remote(view, view, q_s.at[number], q_r.at[number], to)

    q_copies = [
        q_send(x, 0, 0, q_right), q_send(x, 1, 3, q_left),
        q_send(x, 1, 1, q_right), q_send(x, 0, 2, q_left),
    ]
    for copy in q_copies:
        copy.start()

    swap.wait_recv()
    for copy in own_pass(1, 2):
        copy.start()

    for n in range(1, NX):
        table_x(n).wait_recv()

    def table_z(n):
        return remote(table.at[z], table.at[z], tz_s.at[n], tz_r.at[n], (x, zplus(n)))

    for n in range(1, NZ):
        table_z(n).start()

    def split_queries(owner):
        for i in range(NX):
            scaled = qraw[owner, i].astype(F32) * QSCALE
            high = scaled.astype(BF16)
            low = (scaled - high.astype(F32)).astype(BF16)
            qp[owner, i] = jnp.concatenate([high, low], 1)

    split_queries(x)
    for n in range(1, NX):
        acc[xplus(n)] = jnp.zeros((NX, CHUNK, 2 * HD), F32)
        peak[xplus(n)] = jnp.full((NX, CHUNK, HD), LOW, F32)

    def keys_of(block):
        return jnp.concatenate([block[:HD], block[:HD]], 0)

    def values_of(block, live):
        mark = jnp.where(live, 1.0, 0.0).astype(BF16)
        return jnp.concatenate([jnp.concatenate([block[HD:, :HD], block[HD:, HD:]], 0), mark], 1)

    slot_wide = iota((HALF, HD), 0)
    for half, block in enumerate((ring[0, 0], spare[...])):
        kkd[:, half * HALF:(half + 1) * HALF] = keys_of(block)
        vvd[half * HALF:(half + 1) * HALF] = values_of(block, slot_wide + HALF * half < count)
    key_pos = jnp.concatenate(
        [jnp.where(lane + 128 * i < count, kept[i:i + 1], FAR) for i in range(4)], 1
    )
    local_pos = (qpos_ref[...] - c * LOCAL).astype(F32)
    scores = [jnp.dot(qp[x, i], kkd[...], preferred_element_type=F32) for i in range(NX)]
    for i in range(NX):
        own_pos = jnp.sum(
            jnp.where(rank_lane == place + 32 * i, local_pos, 0.0), axis=1, keepdims=True
        ).astype(I32)
        seen_scores = jnp.where(key_pos <= own_pos, scores[i], HIDDEN)
        new_peak = jnp.broadcast_to(
            jnp.maximum(jnp.max(seen_scores, axis=1, keepdims=True), LOW), (CHUNK, HD)
        )
        weights = jnp.exp2(seen_scores - jnp.concatenate([new_peak] * 4, 1)).astype(BF16)
        acc[x, i] = jnp.dot(weights, vvd[...], preferred_element_type=F32)
        peak[x, i] = new_peak

    def owner_row(group):
        return jnp.where(group == 0, x, mirror)

    origins = [z] + [zplus(n if h else NZ - n) for n in (1, 2, 3) for h in (0, 1)] + [zplus(4)]

    def prepare(t, side, group, h):
        block = ring[t, side]
        live_count = lax.div(table[origins[h], x if group == 0 else mirror], ROWS)
        kk[group, h] = keys_of(block)
        vv[group, h * HALF:(h + 1) * HALF] = values_of(block, slot_wide + HALF * group < live_count)

    def poll(t):
        pass_right(t, t).wait_recv()
        pass_left(t, t).wait_recv()
        if t <= 5:
            pass_right(t, t + 2).start()
        if t <= 4 or t == 6:
            pass_left(t, min(t + 2, TILES - 1)).start()
        if t == TILES - 1:
            prepare(t, 0, 0, 7)
            prepare(t, 1, 1, 7)
        else:
            h = t if t % 2 else t - 1
            prepare(t, 0, 1 - t % 2, h)
            prepare(t, 1, 1 - t % 2, h + 1)

    def attend(owner, group, halves):
        row = owner_row(group)
        every = owner > row
        visible = [origins[h] < z for h in halves]
        some = visible[0]
        for v in visible[1:]:
            some = some | v

        def update(bias):
            scores = []
            for i in range(NX):
                parts = [jnp.dot(qp[owner, i], kk[group, h], preferred_element_type=F32) for h in halves]
                if bias is not None:
                    parts = [p + b for p, b in zip(parts, bias)]
                scores.append(parts)
            for i in range(NX):
                old_peak = peak[owner, i]
                top = scores[i][0]
                for p in scores[i][1:]:
                    top = jnp.maximum(top, p)
                new_peak = jnp.maximum(jnp.max(top, axis=1, keepdims=True), old_peak)
                twice = jnp.concatenate([new_peak, new_peak], 1)
                weights = jnp.concatenate([jnp.exp2(p - twice).astype(BF16) for p in scores[i]], 1)
                summed = jnp.dot(
                    weights, vv[group, pl.ds(halves[0] * HALF, len(halves) * HALF)], preferred_element_type=F32
                )
                scale = jnp.exp2(old_peak - new_peak)
                acc[owner, i] = acc[owner, i] * jnp.concatenate([scale, scale], 1) + summed
                peak[owner, i] = new_peak

        @pl.when(every)
        def _():
            update(None)

        @pl.when((owner == row) & some)
        def _():
            update([jnp.where(v, 0.0, HIDDEN) for v in visible])

    def takes_part(source, owner):
        return jnp.minimum(source, NX - 1 - source) <= owner

    def ret(n, owner):
        xd = xplus(n)
        return (
            remote(part.at[owner, xd], got.at[x, owner], ret_s.at[n, owner], ret_r.at[n, owner], (xd, z)),
            remote(partl.at[xd, owner], gotl.at[x, owner], retl_s.at[n, owner], retl_r.at[n, owner], (xd, z)),
        )

    def finish(owner):
        for i in range(NX):
            top = acc[owner, i][:, :HD]
            bottom = acc[owner, i][:, HD:]
            alive = bottom > 0.0
            safe = jnp.where(alive, bottom, 1.0)
            part[owner, i] = (top / safe).astype(BF16)
            logs = jnp.where(alive, peak[owner, i] + jnp.log(safe) * math.log2(math.e), LOW)
            for j in range(2):
                partl[i, owner, j] = jnp.sum(
                    jnp.where(eye, logs[j * 128:(j + 1) * 128], 0.0), axis=0, keepdims=True
                )

        @pl.when(takes_part(x, owner))
        def _():
            for n in range(1, NX):
                for copy in ret(n, owner):
                    copy.start()

        got[x, owner] = part[owner, x]
        gotl[x, owner] = partl[x, owner]

    prepare(0, 0, 0, 0)
    prepare(0, 1, 1, 0)

    def destinations():
        for zz in range(NZ):
            for xx in range(NX):
                slots[zz * NX + xx:zz * NX + xx + 1, :] = lax.rem(table[zz, xx], ROWS).astype(F32)
        wide = iota((128, QROWS), 1)
        pick = jnp.where(iota((128, QROWS), 0) == c * 4 + lax.rem(wide, 4), 1.0, 0.0).astype(BF16)
        picked = jnp.dot(slots[...].astype(BF16), pick, preferred_element_type=F32)
        mine = iota((32, QROWS), 0) == lax.div(iota((32, QROWS), 1), 32)
        slot_of = jnp.sum(jnp.where(mine, picked, 0.0), axis=0, keepdims=True).astype(I32)
        lanes = iota((1, QROWS), 1)
        key = slot_of + ROWS * lax.rem(lax.div(lanes, 4), HEADS)
        for h in range(HEADS):
            hit = iota((ROWS, QROWS), 0) + ROWS * h == key
            ohf[h] = jnp.where(hit, 1.0, 0.0).astype(BF16)

    def early(w, carry):
        @pl.when(w == 0)
        def _():
            for n in range(1, NZ):
                table_z(n).wait_recv()
            poll(1)

        @pl.when(w == 1)
        def _():
            q_send(xplus(NX - 1), 0, 0, q_right).wait_recv()
            q_send(xplus(NX - 1), 0, 4, q_right).start()
            q_send(xplus(1), 1, 3, q_left).wait_recv()
            q_send(xplus(1), 1, 5, q_left).start()
            destinations()
            poll(2)

        @pl.when(w == 2)
        def _():
            q_send(xplus(NX - 1), 1, 1, q_right).wait_recv()
            q_send(xplus(1), 0, 2, q_left).wait_recv()
            split_queries(xplus(1))
            split_queries(xplus(NX - 1))

        @pl.when(w == 4)
        def _():
            poll(3)

        @pl.when(w == 6)
        def _():
            poll(4)
            q_send(xplus(2), 0, 4, q_right).wait_recv()
            q_send(xplus(2), 1, 5, q_left).wait_recv()
            split_queries(xplus(2))

        turn = lax.div(w, 2)
        n = jnp.where(turn == 2, 3, jnp.where(turn == 3, 2, turn))
        attend(xplus(n), lax.rem(w, 2), (0, 1, 2))
        return carry

    lax.fori_loop(0, 2 * NX, early, 0)
    poll(5)

    def late(i, carry):
        @pl.when(i < NX)
        def _():
            def one(group, inner):
                @pl.when((i == 0) & (group == 1))
                def _():
                    poll(6)

                attend(NX - 1 - i, group, (3, 4, 5, 6))
                return inner

            lax.fori_loop(0, 2, one, 0)

        @pl.when(i == 0)
        def _():
            poll(7)

        @pl.when(i >= 1)
        def _():
            def one(group, inner):
                attend(NX - i, group, (7,))
                return inner

            lax.fori_loop(0, 2, one, 0)
            finish(NX - i)

        return carry

    lax.fori_loop(0, NX + 1, late, 0)

    def rows_of(row):
        return jnp.sum(jnp.where(eye, row, 0.0), axis=1, keepdims=True)

    def spread(n, owner):
        zd = zplus(n)
        return remote(fin.at[owner, zd], gath.at[z, owner], a2a_s.at[owner, n], a2a_r.at[owner, n], (x, zd))

    for owner in range(NX - 1, -1, -1):
        sources = [s for s in range(NX) if min(s, NX - 1 - s) <= owner]
        for n in range(1, NX):
            @pl.when(takes_part(xplus(NX - n), owner))
            def _():
                for copy in ret(n, owner):
                    copy.wait_recv()
        logs = [
            jnp.concatenate([rows_of(gotl[s, owner, j]) for j in range(2)], 0) for s in sources
        ]
        most = logs[0]
        for value in logs[1:]:
            most = jnp.maximum(most, value)
        total = jnp.zeros((CHUNK, HD), F32)
        weight = jnp.zeros((CHUNK, 1), F32)
        for s, value in zip(sources, logs):
            share = jnp.exp2(value - most)
            weight = weight + share
            total = total + share * got[s, owner].astype(F32)
        fin[owner] = (total / weight).astype(BF16).reshape(NZ, CHUNK // NZ, HD)
        for n in range(1, NZ):
            spread(n, owner).start()
        gath[z, owner] = fin[owner, z]

    for owner in range(NX - 1, -1, -1):
        for n in range(1, NZ):
            spread(n, owner).wait_recv()
    arrived = gath[...].reshape(QROWS, HD)
    for h in range(HEADS):
        out_ref[:, h * HD:(h + 1) * HD] = jnp.dot(
            ohf[h], arrived, preferred_element_type=F32
        ).astype(BF16)

    swap.wait_send()
    for copy in own_pass(0, 1) + own_pass(1, 2):
        copy.wait_send()
    for t in range(1, 6):
        pass_right(t, t + 2).wait_send()
    for t in (1, 2, 3, 4, 6):
        pass_left(t, min(t + 2, TILES - 1)).wait_send()
    for copy in q_copies:
        copy.wait_send()
    q_send(xplus(NX - 1), 0, 4, q_right).wait_send()
    q_send(xplus(1), 1, 5, q_left).wait_send()
    for n in range(1, NX):
        table_x(n).wait_send()
        for owner in range(NX):
            @pl.when(takes_part(x, owner))
            def _():
                for copy in ret(n, owner):
                    copy.wait_send()
    for n in range(1, NZ):
        table_z(n).wait_send()
        for owner in range(NX):
            spread(n, owner).wait_send()


def per_device(queries, query_pos, k_cache, v_cache, kept_index, kept_count, route):
    dma = pltpu.SemaphoreType.DMA
    vmem = pltpu.VMEM
    anywhere = pl.BlockSpec(memory_space=pl.ANY)
    return pl.pallas_call(
        kernel,
        out_shape=jax.ShapeDtypeStruct((ROWS, QROWS), BF16),
        in_specs=[anywhere] * 6 + [pl.BlockSpec(memory_space=pltpu.SMEM)],
        out_specs=pl.BlockSpec(memory_space=vmem),
        scratch_shapes=[
            vmem((LOCAL, 2 * HD), BF16),
            vmem((SLOTS, LOCAL), BF16),
            vmem((4, 128), I32),
            vmem((1, 128), I32),
            vmem((1, 128), I32),
            vmem((ROWS, QROWS), BF16),
            vmem((HALF, 2 * HD), BF16),
            vmem((TILES, 2, HALF, 2 * HD), BF16),
            vmem((2, TILES, 2 * HD, HALF), BF16),
            vmem((2, TILES * HALF, 2 * HD), BF16),
            vmem((2 * HD, SLOTS), BF16),
            vmem((SLOTS, 2 * HD), BF16),
            vmem((NX, NX, CHUNK, HD), BF16),
            vmem((NX, NX, CHUNK, 2 * HD), BF16),
            vmem((NX, NX, CHUNK, 2 * HD), F32),
            vmem((NX, NX, CHUNK, HD), F32),
            vmem((NX, NX, CHUNK, HD), BF16),
            vmem((NX, NX, 2, 1, 128), F32),
            vmem((NX, NX, CHUNK, HD), BF16),
            vmem((NX, NX, 2, 1, 128), F32),
            vmem((NX, NZ, CHUNK // NZ, HD), BF16),
            vmem((NZ, NX, CHUNK // NZ, HD), BF16),
            vmem((NZ, NX, 1, 128), I32),
            vmem((NZ * NX, 128), F32),
            vmem((HEADS, ROWS, QROWS), BF16),
            dma((4, 2)), dma((4,)), dma, dma,
            dma((TILES, 2)), dma((TILES, 2)),
            dma((6,)), dma((6,)),
            dma((NX, NX)), dma((NX, NX)), dma((NX, NX)), dma((NX, NX)),
            dma((NX, NZ)), dma((NX, NZ)),
            dma((NX,)), dma((NX,)),
            dma((NZ,)), dma((NZ,)),
        ],
        compiler_params=pltpu.CompilerParams(
            collective_id=0, has_side_effects=True, vmem_limit_bytes=56 * 1024 * 1024
        ),
    )(
        kept_index.reshape(4, 128), route.reshape(1, 128), query_pos.reshape(1, 128),
        queries, k_cache, v_cache, kept_count,
    )


def solution(mesh):
    placed = (
        P("context", "mp"),
        P("context"),
        P("context", "mp"),
        P("context", "mp"),
        P("context"),
        P("context"),
        P("context"),
    )
    return jax.shard_map(
        per_device, mesh=mesh, in_specs=placed, out_specs=P("context", "mp"), check_vma=False
    )
```

```python
import math

import jax
import jax.numpy as jnp
from jax import lax
from jax.experimental import pallas as pl
from jax.experimental.pallas import tpu as pltpu
from jax.sharding import PartitionSpec as P

MESH = pl.DeviceIdType.MESH
F32, BF16, I32 = jnp.float32, jnp.bfloat16, jnp.int32

HD = 128
NX = 4
NZ = 8
ROWS = 128
HEADS = 8
SLOTS = 512
HALF = SLOTS // 2
LOCAL = 4096
QROWS = ROWS * HEADS
CHUNK = QROWS // NX
TILES = 8
FAR = 1 << 29
LOW = -1e30
HIDDEN = -2e30
QSCALE = math.log2(math.e) / math.sqrt(HD)


def iota(shape, axis):
    return lax.broadcasted_iota(I32, shape, axis)


def kernel(
    idx_hbm, route_hbm, qpos_hbm, q_hbm, k_hbm, v_hbm, count_ref, out_ref,
    cache, hot, idx_ref, route_ref, qpos_ref, q_ref,
    spare, ring, kk, vv, kkd, vvd, qraw, qp, acc, peak, part, partl, got, gotl, fin, gath,
    table, slots, ohf,
    load_sem, small_sem, swap_s, swap_r, ring_s, ring_r, q_s, q_r, ret_s, ret_r, retl_s, retl_r,
    a2a_s, a2a_r, tx_s, tx_r, tz_s, tz_r,
):
    c = lax.axis_index("context")
    x = lax.div(c, NZ)
    z = lax.rem(c, NZ)
    mirror = NX - 1 - x
    right, left = (x, lax.rem(z + 1, NZ)), (x, lax.rem(z + NZ - 1, NZ))

    def at(where):
        return {"context": where[0] * NZ + where[1]}

    def xplus(n):
        return lax.rem(x + n, NX)

    def zplus(n):
        return lax.rem(z + n, NZ)

    def remote(src, dst, send, recv, to):
        return pltpu.make_async_remote_copy(
            src_ref=src, dst_ref=dst, send_sem=send, recv_sem=recv, device_id=at(to), device_id_type=MESH
        )

    smalls = []
    for i, (src, dst) in enumerate(
        ((idx_hbm, idx_ref), (route_hbm, route_ref), (qpos_hbm, qpos_ref), (q_hbm, q_ref))
    ):
        copy = pltpu.make_async_copy(src, dst, small_sem.at[i])
        copy.start()
        smalls.append(copy)
    loads = []
    for i in range(4):
        rows = pl.ds(i * 1024, 1024)
        for side, ref in enumerate((k_hbm, v_hbm)):
            copy = pltpu.make_async_copy(
                ref.at[rows], cache.at[rows, pl.ds(side * HD, HD)], load_sem.at[i, side]
            )
            copy.start()
            loads.append(copy)

    barrier = pltpu.get_barrier_semaphore()
    for n in range(1, NX):
        pl.semaphore_signal(barrier, inc=1, device_id=at((xplus(n), z)), device_id_type=MESH)
    for n in range(1, NZ):
        pl.semaphore_signal(barrier, inc=1, device_id=at((x, zplus(n))), device_id_type=MESH)

    count = count_ref[0]
    eye = iota((128, 128), 0) == iota((128, 128), 1)
    lane = iota((1, 128), 1)

    def column(row):
        return jnp.sum(jnp.where(eye, row.astype(F32), 0.0), axis=1, keepdims=True).astype(I32)

    for copy in smalls[:3]:
        copy.wait()
    kept = idx_ref[...]
    repeat = jnp.broadcast_to(kept[0:1, 0:1], (1, 128))
    for i in (2, 3, 0, 1):
        index = column(jnp.where(lane + 128 * i < count, kept[i:i + 1], repeat))
        for j in range(4):
            hit = iota((128, 1024), 1) == index - 1024 * j
            hot[i * 128:(i + 1) * 128, j * 1024:(j + 1) * 1024] = jnp.where(hit, 1.0, 0.0).astype(BF16)

    route_lane = route_ref[...]
    dest_lane = lax.div(route_lane, ROWS)
    dest_col = column(dest_lane)
    same = dest_col == dest_lane
    first = iota((128, 128), 0)
    second = iota((128, 128), 1)
    before_lane = jnp.sum(jnp.where(same & (first < second), 1.0, 0.0), axis=0, keepdims=True).astype(I32)
    before_col = jnp.sum(jnp.where(same & (second < first), 1.0, 0.0), axis=1, keepdims=True).astype(I32)
    rank_lane = dest_lane * (ROWS // (NX * NZ)) + before_lane
    rank_col = dest_col * (ROWS // (NX * NZ)) + before_col
    slot_col = column(lax.rem(route_lane, ROWS)).astype(F32)
    slot_row = jnp.sum(jnp.where(rank_col == second, slot_col, 0.0), axis=0, keepdims=True).astype(I32)
    table[z, x] = slot_row + ROWS * count

    def gather(half):
        total = jnp.dot(hot[half * HALF:(half + 1) * HALF, :], cache[...], preferred_element_type=F32)
        live = iota((HALF, HD), 0) + HALF * half < count
        keys = jnp.transpose(total[:, :HD].astype(BF16))
        values = jnp.where(live, total[:, HD:], 0.0).astype(BF16)
        return jnp.concatenate([keys, jnp.concatenate([values[:HD], values[HD:]], 1)], 0)

    for copy in loads:
        copy.wait()
    spare[...] = gather(1)
    pl.semaphore_wait(barrier, NX - 1 + NZ - 1)
    swap = remote(spare, ring.at[0, 1], swap_s, swap_r, (mirror, z))
    swap.start()
    ring[0, 0] = gather(0)

    def pass_right(source, target):
        return remote(ring.at[source, 0], ring.at[target, 0], ring_s.at[target, 0], ring_r.at[target, 0], right)

    def pass_left(source, target):
        return remote(ring.at[source, 1], ring.at[target, 1], ring_s.at[target, 1], ring_r.at[target, 1], left)

    def own_pass(half, target):
        return (
            remote(ring.at[0, half], ring.at[target, 0], ring_s.at[target, 0], ring_r.at[target, 0], right),
            remote(ring.at[0, half], ring.at[target, 1], ring_s.at[target, 1], ring_r.at[target, 1], left),
        )

    for copy in own_pass(0, 1):
        copy.start()

    def table_x(n):
        return remote(table.at[z, x], table.at[z, x], tx_s.at[n], tx_r.at[n], (xplus(n), z))

    for n in range(1, NX):
        table_x(n).start()

    smalls[3].wait()
    stacked = jnp.concatenate([q_ref[:, h * HD:(h + 1) * HD] for h in range(HEADS)], 0)
    rank_key = jnp.concatenate([rank_lane + ROWS * h for h in range(HEADS)], 1)
    within = iota((CHUNK, 1), 0)
    place = lax.div(within, 32) * 4 + lax.rem(within, 4)
    head_of = lax.rem(lax.div(within, 4), HEADS)
    for i in range(NX):
        hit = rank_key == place + 32 * i + ROWS * head_of
        one = jnp.where(hit, 1.0, 0.0).astype(BF16)
        qraw[x, i] = jnp.dot(one, stacked, preferred_element_type=F32).astype(BF16)

    q_right, q_left = (xplus(1), z), (xplus(NX - 1), z)

    def q_send(owner, half, number, to):
        view = qraw.at[owner, pl.ds(2 * half, 2)]
        return remote(view, view, q_s.at[number], q_r.at[number], to)

    q_copies = [
        q_send(x, 0, 0, q_right), q_send(x, 1, 3, q_left),
        q_send(x, 1, 1, q_right), q_send(x, 0, 2, q_left),
    ]
    for copy in q_copies:
        copy.start()

    swap.wait_recv()
    for copy in own_pass(1, 2):
        copy.start()

    for n in range(1, NX):
        table_x(n).wait_recv()

    def table_z(n):
        return remote(table.at[z], table.at[z], tz_s.at[n], tz_r.at[n], (x, zplus(n)))

    for n in range(1, NZ):
        table_z(n).start()

    def split_queries(owner):
        for i in range(NX):
            scaled = qraw[owner, i].astype(F32) * QSCALE
            high = scaled.astype(BF16)
            low = (scaled - high.astype(F32)).astype(BF16)
            qp[owner, i] = jnp.concatenate([high, low], 1)

    split_queries(x)
    for n in range(1, NX):
        acc[xplus(n)] = jnp.zeros((NX, CHUNK, 2 * HD), F32)
        peak[xplus(n)] = jnp.full((NX, CHUNK, HD), LOW, F32)

    def keys_of(block):
        return jnp.concatenate([block[:HD], block[:HD]], 0)

    def values_of(block, live):
        mark = jnp.where(live, 1.0, 0.0).astype(BF16)
        return jnp.concatenate([jnp.concatenate([block[HD:, :HD], block[HD:, HD:]], 0), mark], 1)

    slot_wide = iota((HALF, HD), 0)
    for half, block in enumerate((ring[0, 0], spare[...])):
        kkd[:, half * HALF:(half + 1) * HALF] = keys_of(block)
        vvd[half * HALF:(half + 1) * HALF] = values_of(block, slot_wide + HALF * half < count)
    key_pos = jnp.concatenate(
        [jnp.where(lane + 128 * i < count, kept[i:i + 1], FAR) for i in range(4)], 1
    )
    local_pos = (qpos_ref[...] - c * LOCAL).astype(F32)
    scores = [jnp.dot(qp[x, i], kkd[...], preferred_element_type=F32) for i in range(NX)]
    for i in range(NX):
        own_pos = jnp.sum(
            jnp.where(rank_lane == place + 32 * i, local_pos, 0.0), axis=1, keepdims=True
        ).astype(I32)
        seen_scores = jnp.where(key_pos <= own_pos, scores[i], HIDDEN)
        new_peak = jnp.broadcast_to(
            jnp.maximum(jnp.max(seen_scores, axis=1, keepdims=True), LOW), (CHUNK, HD)
        )
        weights = jnp.exp2(seen_scores - jnp.concatenate([new_peak] * 4, 1)).astype(BF16)
        acc[x, i] = jnp.dot(weights, vvd[...], preferred_element_type=F32)
        peak[x, i] = new_peak

    def owner_row(group):
        return jnp.where(group == 0, x, mirror)

    def origin_of(h):
        step = lax.div(h + 1, 2)
        return lax.rem(jnp.where(lax.rem(h, 2) == 1, z + NZ - step, z + step), NZ)

    def prepare(t, side, group, h):
        block = ring[t, side]
        live_count = lax.div(table[origin_of(h), owner_row(group)], ROWS)
        kk[group, h] = keys_of(block)
        vv[group, pl.ds(h * HALF, HALF)] = values_of(block, slot_wide + HALF * group < live_count)

    def forward(t):
        pass_right(t, t).wait_recv()
        pass_left(t, t).wait_recv()

        @pl.when(t <= 5)
        def _():
            pass_right(t, t + 2).start()

        @pl.when((t <= 4) | (t == 6))
        def _():
            pass_left(t, jnp.minimum(t + 2, TILES - 1)).start()

    def arrange(t):
        end = t == TILES - 1
        group = 1 - lax.rem(t, 2)
        h = t - group
        prepare(t, 0, group, h)
        prepare(t, 1, jnp.where(end, 1, group), jnp.where(end, h, h + 1))

    def attend(owner, group, start, number):
        halves = [start + k for k in range(number)]
        row = owner_row(group)
        every = owner > row
        visible = [origin_of(h) < z for h in halves]
        some = visible[0]
        for v in visible[1:]:
            some = some | v

        def update(bias):
            scores = []
            for i in range(NX):
                parts = [jnp.dot(qp[owner, i], kk[group, h], preferred_element_type=F32) for h in halves]
                if bias is not None:
                    parts = [p + b for p, b in zip(parts, bias)]
                scores.append(parts)
            for i in range(NX):
                old_peak = peak[owner, i]
                top = scores[i][0]
                for p in scores[i][1:]:
                    top = jnp.maximum(top, p)
                new_peak = jnp.maximum(jnp.max(top, axis=1, keepdims=True), old_peak)
                twice = jnp.concatenate([new_peak, new_peak], 1)
                weights = jnp.concatenate([jnp.exp2(p - twice).astype(BF16) for p in scores[i]], 1)
                summed = jnp.dot(
                    weights, vv[group, pl.ds(start * HALF, number * HALF)], preferred_element_type=F32
                )
                scale = jnp.exp2(old_peak - new_peak)
                acc[owner, i] = acc[owner, i] * jnp.concatenate([scale, scale], 1) + summed
                peak[owner, i] = new_peak

        @pl.when(every)
        def _():
            update(None)

        @pl.when((owner == row) & some)
        def _():
            update([jnp.where(v, 0.0, HIDDEN) for v in visible])

    def takes_part(source, owner):
        return jnp.minimum(source, NX - 1 - source) <= owner

    def ret(n, owner):
        xd = xplus(n)
        return (
            remote(part.at[owner, xd], got.at[x, owner], ret_s.at[n, owner], ret_r.at[n, owner], (xd, z)),
            remote(partl.at[xd, owner], gotl.at[x, owner], retl_s.at[n, owner], retl_r.at[n, owner], (xd, z)),
        )

    def finish(owner):
        for i in range(NX):
            top = acc[owner, i][:, :HD]
            bottom = acc[owner, i][:, HD:]
            alive = bottom > 0.0
            safe = jnp.where(alive, bottom, 1.0)
            part[owner, i] = (top / safe).astype(BF16)
            logs = jnp.where(alive, peak[owner, i] + jnp.log(safe) * math.log2(math.e), LOW)
            for j in range(2):
                partl[i, owner, j] = jnp.sum(
                    jnp.where(eye, logs[j * 128:(j + 1) * 128], 0.0), axis=0, keepdims=True
                )

        @pl.when(takes_part(x, owner))
        def _():
            for n in range(1, NX):
                for copy in ret(n, owner):
                    copy.start()

        got[x, owner] = part[owner, x]
        gotl[x, owner] = partl[x, owner]

    prepare(0, 0, 0, 0)
    prepare(0, 1, 1, 0)

    def destinations():
        for zz in range(NZ):
            for xx in range(NX):
                slots[zz * NX + xx:zz * NX + xx + 1, :] = lax.rem(table[zz, xx], ROWS).astype(F32)
        wide = iota((128, QROWS), 1)
        pick = jnp.where(iota((128, QROWS), 0) == c * 4 + lax.rem(wide, 4), 1.0, 0.0).astype(BF16)
        picked = jnp.dot(slots[...].astype(BF16), pick, preferred_element_type=F32)
        mine = iota((32, QROWS), 0) == lax.div(iota((32, QROWS), 1), 32)
        slot_of = jnp.sum(jnp.where(mine, picked, 0.0), axis=0, keepdims=True).astype(I32)
        lanes = iota((1, QROWS), 1)
        key = slot_of + ROWS * lax.rem(lax.div(lanes, 4), HEADS)
        for h in range(HEADS):
            hit = iota((ROWS, QROWS), 0) + ROWS * h == key
            ohf[h] = jnp.where(hit, 1.0, 0.0).astype(BF16)

    def early(w, carry):
        @pl.when(w == 0)
        def _():
            forward(1)
            for n in range(1, NZ):
                table_z(n).wait_recv()
            arrange(1)

        @pl.when(w == 1)
        def _():
            q_send(xplus(NX - 1), 0, 0, q_right).wait_recv()
            q_send(xplus(NX - 1), 0, 4, q_right).start()
            q_send(xplus(1), 1, 3, q_left).wait_recv()
            q_send(xplus(1), 1, 5, q_left).start()
            destinations()
            forward(2)
            arrange(2)

        @pl.when(w == 2)
        def _():
            q_send(xplus(NX - 1), 1, 1, q_right).wait_recv()
            q_send(xplus(1), 0, 2, q_left).wait_recv()
            split_queries(xplus(1))
            split_queries(xplus(NX - 1))

        @pl.when(w == 5)
        def _():
            forward(3)
            arrange(3)

        @pl.when(w == 6)
        def _():
            q_send(xplus(2), 0, 4, q_right).wait_recv()
            q_send(xplus(2), 1, 5, q_left).wait_recv()
            split_queries(xplus(2))

        turn = lax.div(w, 2)
        n = jnp.where(turn == 2, 3, jnp.where(turn == 3, 2, turn))
        attend(xplus(n), lax.rem(w, 2), 0, 3)
        return carry

    lax.fori_loop(0, 2 * NX, early, 0)

    def middle(t, carry):
        group = 1 - lax.rem(t, 2)

        def one(i, inner):
            @pl.when(i == 2)
            def _():
                forward(t + 1)
                arrange(t + 1)

            attend(NX - 1 - i, group, t - group, 2)
            return inner

        lax.fori_loop(0, NX, one, 0)
        return carry

    lax.fori_loop(3, TILES - 1, middle, 0)

    def late(i, carry):
        owner = NX - 1 - i

        def one(group, inner):
            attend(owner, group, TILES - 1, 1)
            return inner

        lax.fori_loop(0, 2, one, 0)
        finish(owner)
        return carry

    lax.fori_loop(0, NX, late, 0)

    def rows_of(row):
        return jnp.sum(jnp.where(eye, row, 0.0), axis=1, keepdims=True)

    def spread(n, owner):
        zd = zplus(n)
        return remote(fin.at[owner, zd], gath.at[z, owner], a2a_s.at[owner, n], a2a_r.at[owner, n], (x, zd))

    for owner in range(NX - 1, -1, -1):
        sources = [s for s in range(NX) if min(s, NX - 1 - s) <= owner]
        for n in range(1, NX):
            @pl.when(takes_part(xplus(NX - n), owner))
            def _():
                for copy in ret(n, owner):
                    copy.wait_recv()
        logs = [
            jnp.concatenate([rows_of(gotl[s, owner, j]) for j in range(2)], 0) for s in sources
        ]
        most = logs[0]
        for value in logs[1:]:
            most = jnp.maximum(most, value)
        total = jnp.zeros((CHUNK, HD), F32)
        weight = jnp.zeros((CHUNK, 1), F32)
        for s, value in zip(sources, logs):
            share = jnp.exp2(value - most)
            weight = weight + share
            total = total + share * got[s, owner].astype(F32)
        fin[owner] = (total / weight).astype(BF16).reshape(NZ, CHUNK // NZ, HD)
        for n in range(1, NZ):
            spread(n, owner).start()
        gath[z, owner] = fin[owner, z]

    for owner in range(NX - 1, -1, -1):
        for n in range(1, NZ):
            spread(n, owner).wait_recv()
    arrived = gath[...].reshape(QROWS, HD)
    for h in range(HEADS):
        out_ref[:, h * HD:(h + 1) * HD] = jnp.dot(
            ohf[h], arrived, preferred_element_type=F32
        ).astype(BF16)

    swap.wait_send()
    for copy in own_pass(0, 1) + own_pass(1, 2):
        copy.wait_send()
    for t in range(1, 6):
        pass_right(t, t + 2).wait_send()
    for t in (1, 2, 3, 4, 6):
        pass_left(t, min(t + 2, TILES - 1)).wait_send()
    for copy in q_copies:
        copy.wait_send()
    q_send(xplus(NX - 1), 0, 4, q_right).wait_send()
    q_send(xplus(1), 1, 5, q_left).wait_send()
    for n in range(1, NX):
        table_x(n).wait_send()
        for owner in range(NX):
            @pl.when(takes_part(x, owner))
            def _():
                for copy in ret(n, owner):
                    copy.wait_send()
    for n in range(1, NZ):
        table_z(n).wait_send()
        for owner in range(NX):
            spread(n, owner).wait_send()


def per_device(queries, query_pos, k_cache, v_cache, kept_index, kept_count, route):
    dma = pltpu.SemaphoreType.DMA
    vmem = pltpu.VMEM
    anywhere = pl.BlockSpec(memory_space=pl.ANY)
    return pl.pallas_call(
        kernel,
        out_shape=pltpu.VMEM((ROWS, QROWS), BF16),
        in_specs=[anywhere] * 6 + [pl.BlockSpec(memory_space=pltpu.SMEM)],
        out_specs=pl.BlockSpec(memory_space=vmem),
        scratch_shapes=[
            vmem((LOCAL, 2 * HD), BF16),
            vmem((SLOTS, LOCAL), BF16),
            vmem((4, 128), I32),
            vmem((1, 128), I32),
            vmem((1, 128), I32),
            vmem((ROWS, QROWS), BF16),
            vmem((HALF, 2 * HD), BF16),
            vmem((TILES, 2, HALF, 2 * HD), BF16),
            vmem((2, TILES, 2 * HD, HALF), BF16),
            vmem((2, TILES * HALF, 2 * HD), BF16),
            vmem((2 * HD, SLOTS), BF16),
            vmem((SLOTS, 2 * HD), BF16),
            vmem((NX, NX, CHUNK, HD), BF16),
            vmem((NX, NX, CHUNK, 2 * HD), BF16),
            vmem((NX, NX, CHUNK, 2 * HD), F32),
            vmem((NX, NX, CHUNK, HD), F32),
            vmem((NX, NX, CHUNK, HD), BF16),
            vmem((NX, NX, 2, 1, 128), F32),
            vmem((NX, NX, CHUNK, HD), BF16),
            vmem((NX, NX, 2, 1, 128), F32),
            vmem((NX, NZ, CHUNK // NZ, HD), BF16),
            vmem((NZ, NX, CHUNK // NZ, HD), BF16),
            vmem((NZ, NX, 1, 128), I32),
            vmem((NZ * NX, 128), F32),
            vmem((HEADS, ROWS, QROWS), BF16),
            dma((4, 2)), dma((4,)), dma, dma,
            dma((TILES, 2)), dma((TILES, 2)),
            dma((6,)), dma((6,)),
            dma((NX, NX)), dma((NX, NX)), dma((NX, NX)), dma((NX, NX)),
            dma((NX, NZ)), dma((NX, NZ)),
            dma((NX,)), dma((NX,)),
            dma((NZ,)), dma((NZ,)),
        ],
        compiler_params=pltpu.CompilerParams(
            collective_id=0, has_side_effects=True, vmem_limit_bytes=56 * 1024 * 1024
        ),
    )(
        kept_index.reshape(4, 128), route.reshape(1, 128), query_pos.reshape(1, 128),
        queries, k_cache, v_cache, kept_count,
    )


def solution(mesh):
    placed = (
        P("context", "mp"),
        P("context"),
        P("context", "mp"),
        P("context", "mp"),
        P("context"),
        P("context"),
        P("context"),
    )
    return jax.shard_map(
        per_device, mesh=mesh, in_specs=placed, out_specs=P("context", "mp"), check_vma=False
    )
```

```python
import math

import jax
import jax.numpy as jnp
from jax import lax
from jax.experimental import pallas as pl
from jax.experimental.pallas import tpu as pltpu
from jax.sharding import PartitionSpec as P

MESH = pl.DeviceIdType.MESH
F32, BF16, I32 = jnp.float32, jnp.bfloat16, jnp.int32

HD = 128
NX = 4
NZ = 8
ROWS = 128
HEADS = 8
SLOTS = 512
HALF = SLOTS // 2
LOCAL = 4096
QROWS = ROWS * HEADS
CHUNK = QROWS // NX
TILES = 8
FAR = 1 << 29
LOW = -1e30
HIDDEN = -2e30
QSCALE = math.log2(math.e) / math.sqrt(HD)


def iota(shape, axis):
    return lax.broadcasted_iota(I32, shape, axis)


def kernel(
    idx_hbm, route_hbm, qpos_hbm, q_hbm, k_hbm, v_hbm, count_ref, out_ref,
    cache, hot, idx_ref, route_ref, qpos_ref, q_ref,
    spare, ring, kk, vv, kkd, vvd, qraw, qp, acc, peak, part, partl, got, gotl, fin, gath,
    table, slots, ohf,
    load_sem, small_sem, swap_s, swap_r, ring_s, ring_r, q_s, q_r, ret_s, ret_r, retl_s, retl_r,
    a2a_s, a2a_r, tx_s, tx_r, tz_s, tz_r,
):
    c = lax.axis_index("context")
    x = lax.div(c, NZ)
    z = lax.rem(c, NZ)
    mirror = NX - 1 - x
    right, left = (x, lax.rem(z + 1, NZ)), (x, lax.rem(z + NZ - 1, NZ))

    def at(where):
        return {"context": where[0] * NZ + where[1]}

    def xplus(n):
        return lax.rem(x + n, NX)

    def zplus(n):
        return lax.rem(z + n, NZ)

    def remote(src, dst, send, recv, to):
        return pltpu.make_async_remote_copy(
            src_ref=src, dst_ref=dst, send_sem=send, recv_sem=recv, device_id=at(to), device_id_type=MESH
        )

    smalls = []
    for i, (src, dst) in enumerate(
        ((idx_hbm, idx_ref), (route_hbm, route_ref), (qpos_hbm, qpos_ref), (q_hbm, q_ref))
    ):
        copy = pltpu.make_async_copy(src, dst, small_sem.at[i])
        copy.start()
        smalls.append(copy)
    loads = []
    for i in range(4):
        rows = pl.ds(i * 1024, 1024)
        for side, ref in enumerate((k_hbm, v_hbm)):
            copy = pltpu.make_async_copy(
                ref.at[rows], cache.at[rows, pl.ds(side * HD, HD)], load_sem.at[i, side]
            )
            copy.start()
            loads.append(copy)

    barrier = pltpu.get_barrier_semaphore()
    for n in range(1, NX):
        pl.semaphore_signal(barrier, inc=1, device_id=at((xplus(n), z)), device_id_type=MESH)
    for n in range(1, NZ):
        pl.semaphore_signal(barrier, inc=1, device_id=at((x, zplus(n))), device_id_type=MESH)

    count = count_ref[0]
    eye = iota((128, 128), 0) == iota((128, 128), 1)
    lane = iota((1, 128), 1)

    def column(row):
        return jnp.sum(jnp.where(eye, row.astype(F32), 0.0), axis=1, keepdims=True).astype(I32)

    for copy in smalls[:3]:
        copy.wait()
    kept = idx_ref[...]
    repeat = jnp.broadcast_to(kept[0:1, 0:1], (1, 128))
    for i in (2, 3, 0, 1):
        index = column(jnp.where(lane + 128 * i < count, kept[i:i + 1], repeat))
        for j in range(4):
            hit = iota((128, 1024), 1) == index - 1024 * j
            hot[i * 128:(i + 1) * 128, j * 1024:(j + 1) * 1024] = jnp.where(hit, 1.0, 0.0).astype(BF16)

    route_lane = route_ref[...]
    dest_lane = lax.div(route_lane, ROWS)
    dest_col = column(dest_lane)
    same = dest_col == dest_lane
    first = iota((128, 128), 0)
    second = iota((128, 128), 1)
    before_lane = jnp.sum(jnp.where(same & (first < second), 1.0, 0.0), axis=0, keepdims=True).astype(I32)
    before_col = jnp.sum(jnp.where(same & (second < first), 1.0, 0.0), axis=1, keepdims=True).astype(I32)
    rank_lane = dest_lane * (ROWS // (NX * NZ)) + before_lane
    rank_col = dest_col * (ROWS // (NX * NZ)) + before_col
    slot_col = column(lax.rem(route_lane, ROWS)).astype(F32)
    slot_row = jnp.sum(jnp.where(rank_col == second, slot_col, 0.0), axis=0, keepdims=True).astype(I32)
    table[z, x] = slot_row + ROWS * count

    def gather(half):
        total = jnp.dot(hot[half * HALF:(half + 1) * HALF, :], cache[...], preferred_element_type=F32)
        live = iota((HALF, HD), 0) + HALF * half < count
        keys = jnp.transpose(total[:, :HD].astype(BF16))
        values = jnp.where(live, total[:, HD:], 0.0).astype(BF16)
        return jnp.concatenate([keys, jnp.concatenate([values[:HD], values[HD:]], 1)], 0)

    for copy in loads:
        copy.wait()
    spare[...] = gather(1)
    pl.semaphore_wait(barrier, NX - 1 + NZ - 1)
    swap = remote(spare, ring.at[0, 1], swap_s, swap_r, (mirror, z))
    swap.start()
    ring[0, 0] = gather(0)

    def pass_right(source, target):
        return remote(ring.at[source, 0], ring.at[target, 0], ring_s.at[target, 0], ring_r.at[target, 0], right)

    def pass_left(source, target):
        return remote(ring.at[source, 1], ring.at[target, 1], ring_s.at[target, 1], ring_r.at[target, 1], left)

    def own_pass(half, target):
        return (
            remote(ring.at[0, half], ring.at[target, 0], ring_s.at[target, 0], ring_r.at[target, 0], right),
            remote(ring.at[0, half], ring.at[target, 1], ring_s.at[target, 1], ring_r.at[target, 1], left),
        )

    for copy in own_pass(0, 1):
        copy.start()

    def table_x(n):
        return remote(table.at[z, x], table.at[z, x], tx_s.at[n], tx_r.at[n], (xplus(n), z))

    for n in range(1, NX):
        table_x(n).start()

    smalls[3].wait()
    stacked = jnp.concatenate([q_ref[:, h * HD:(h + 1) * HD] for h in range(HEADS)], 0)
    rank_key = jnp.concatenate([rank_lane + ROWS * h for h in range(HEADS)], 1)
    within = iota((CHUNK, 1), 0)
    place = lax.div(within, 32) * 4 + lax.rem(within, 4)
    head_of = lax.rem(lax.div(within, 4), HEADS)
    for i in range(NX):
        hit = rank_key == place + 32 * i + ROWS * head_of
        one = jnp.where(hit, 1.0, 0.0).astype(BF16)
        qraw[x, i] = jnp.dot(one, stacked, preferred_element_type=F32).astype(BF16)

    q_right, q_left = (xplus(1), z), (xplus(NX - 1), z)

    def q_send(owner, half, number, to):
        view = qraw.at[owner, pl.ds(2 * half, 2)]
        return remote(view, view, q_s.at[number], q_r.at[number], to)

    q_copies = [
        q_send(x, 0, 0, q_right), q_send(x, 1, 3, q_left),
        q_send(x, 1, 1, q_right), q_send(x, 0, 2, q_left),
    ]
    for copy in q_copies:
        copy.start()

    def split_queries(owner):
        for i in range(NX):
            scaled = qraw[owner, i].astype(F32) * QSCALE
            high = scaled.astype(BF16)
            low = (scaled - high.astype(F32)).astype(BF16)
            qp[owner, i] = jnp.concatenate([high, low], 1)

    split_queries(x)
    for n in range(1, NX):
        acc[xplus(n)] = jnp.zeros((NX, CHUNK, 2 * HD), F32)
        peak[xplus(n)] = jnp.full((NX, CHUNK, HD), LOW, F32)

    def keys_of(block):
        return jnp.concatenate([block[:HD], block[:HD]], 0)

    def values_of(block, live):
        mark = jnp.where(live, 1.0, 0.0).astype(BF16)
        return jnp.concatenate([jnp.concatenate([block[HD:, :HD], block[HD:, HD:]], 0), mark], 1)

    slot_wide = iota((HALF, HD), 0)
    for half, block in enumerate((ring[0, 0], spare[...])):
        kkd[:, half * HALF:(half + 1) * HALF] = keys_of(block)
        vvd[half * HALF:(half + 1) * HALF] = values_of(block, slot_wide + HALF * half < count)
    key_pos = jnp.concatenate(
        [jnp.where(lane + 128 * i < count, kept[i:i + 1], FAR) for i in range(4)], 1
    )
    local_pos = (qpos_ref[...] - c * LOCAL).astype(F32)
    scores = [jnp.dot(qp[x, i], kkd[...], preferred_element_type=F32) for i in range(NX)]
    for i in range(NX):
        own_pos = jnp.sum(
            jnp.where(rank_lane == place + 32 * i, local_pos, 0.0), axis=1, keepdims=True
        ).astype(I32)
        seen_scores = jnp.where(key_pos <= own_pos, scores[i], HIDDEN)
        new_peak = jnp.broadcast_to(
            jnp.maximum(jnp.max(seen_scores, axis=1, keepdims=True), LOW), (CHUNK, HD)
        )
        weights = jnp.exp2(seen_scores - jnp.concatenate([new_peak] * 4, 1)).astype(BF16)
        acc[x, i] = jnp.dot(weights, vvd[...], preferred_element_type=F32)
        peak[x, i] = new_peak

    for n in range(1, NX):
        table_x(n).wait_recv()

    def table_z(n):
        return remote(table.at[z], table.at[z], tz_s.at[n], tz_r.at[n], (x, zplus(n)))

    for n in range(1, NZ):
        table_z(n).start()

    swap.wait_recv()
    for copy in own_pass(1, 2):
        copy.start()

    def owner_row(group):
        return jnp.where(group == 0, x, mirror)

    def origin_of(h):
        step = lax.div(h + 1, 2)
        return lax.rem(jnp.where(lax.rem(h, 2) == 1, z + NZ - step, z + step), NZ)

    def prepare(t, side, group, h):
        block = ring[t, side]
        live_count = lax.div(table[origin_of(h), owner_row(group)], ROWS)
        kk[group, h] = keys_of(block)
        vv[group, pl.ds(h * HALF, HALF)] = values_of(block, slot_wide + HALF * group < live_count)

    def forward(t):
        pass_right(t, t).wait_recv()
        pass_left(t, t).wait_recv()

        @pl.when(t <= 5)
        def _():
            pass_right(t, t + 2).start()

        @pl.when((t <= 4) | (t == 6))
        def _():
            pass_left(t, jnp.minimum(t + 2, TILES - 1)).start()

    def arrange(t):
        end = t == TILES - 1
        group = 1 - lax.rem(t, 2)
        h = t - group
        prepare(t, 0, group, h)
        prepare(t, 1, jnp.where(end, 1, group), jnp.where(end, h, h + 1))

    def attend(owner, group, start, number):
        halves = [start + k for k in range(number)]
        row = owner_row(group)
        every = owner > row
        visible = [origin_of(h) < z for h in halves]
        some = visible[0]
        for v in visible[1:]:
            some = some | v

        def update(bias):
            scores = []
            for i in range(NX):
                parts = [jnp.dot(qp[owner, i], kk[group, h], preferred_element_type=F32) for h in halves]
                if bias is not None:
                    parts = [p + b for p, b in zip(parts, bias)]
                scores.append(parts)
            for i in range(NX):
                old_peak = peak[owner, i]
                top = scores[i][0]
                for p in scores[i][1:]:
                    top = jnp.maximum(top, p)
                new_peak = jnp.maximum(jnp.max(top, axis=1, keepdims=True), old_peak)
                twice = jnp.concatenate([new_peak, new_peak], 1)
                weights = jnp.concatenate([jnp.exp2(p - twice).astype(BF16) for p in scores[i]], 1)
                summed = jnp.dot(
                    weights, vv[group, pl.ds(start * HALF, number * HALF)], preferred_element_type=F32
                )
                scale = jnp.exp2(old_peak - new_peak)
                acc[owner, i] = acc[owner, i] * jnp.concatenate([scale, scale], 1) + summed
                peak[owner, i] = new_peak

        @pl.when(every)
        def _():
            update(None)

        @pl.when((owner == row) & some)
        def _():
            update([jnp.where(v, 0.0, HIDDEN) for v in visible])

    def takes_part(source, owner):
        return jnp.minimum(source, NX - 1 - source) <= owner

    def ret(n, owner):
        xd = xplus(n)
        return (
            remote(part.at[owner, xd], got.at[x, owner], ret_s.at[n, owner], ret_r.at[n, owner], (xd, z)),
            remote(partl.at[xd, owner], gotl.at[x, owner], retl_s.at[n, owner], retl_r.at[n, owner], (xd, z)),
        )

    def finish(owner):
        for i in range(NX):
            top = acc[owner, i][:, :HD]
            bottom = acc[owner, i][:, HD:]
            alive = bottom > 0.0
            safe = jnp.where(alive, bottom, 1.0)
            part[owner, i] = (top / safe).astype(BF16)
            logs = jnp.where(alive, peak[owner, i] + jnp.log(safe) * math.log2(math.e), LOW)
            for j in range(2):
                partl[i, owner, j] = jnp.sum(
                    jnp.where(eye, logs[j * 128:(j + 1) * 128], 0.0), axis=0, keepdims=True
                )

        @pl.when(takes_part(x, owner))
        def _():
            for n in range(1, NX):
                for copy in ret(n, owner):
                    copy.start()

        got[x, owner] = part[owner, x]
        gotl[x, owner] = partl[x, owner]

    prepare(0, 0, 0, 0)
    prepare(0, 1, 1, 0)

    def destinations():
        for zz in range(NZ):
            for xx in range(NX):
                slots[zz * NX + xx:zz * NX + xx + 1, :] = lax.rem(table[zz, xx], ROWS).astype(F32)
        wide = iota((128, QROWS), 1)
        pick = jnp.where(iota((128, QROWS), 0) == c * 4 + lax.rem(wide, 4), 1.0, 0.0).astype(BF16)
        picked = jnp.dot(slots[...].astype(BF16), pick, preferred_element_type=F32)
        mine = iota((32, QROWS), 0) == lax.div(iota((32, QROWS), 1), 32)
        slot_of = jnp.sum(jnp.where(mine, picked, 0.0), axis=0, keepdims=True).astype(I32)
        lanes = iota((1, QROWS), 1)
        key = slot_of + ROWS * lax.rem(lax.div(lanes, 4), HEADS)
        for h in range(HEADS):
            hit = iota((ROWS, QROWS), 0) + ROWS * h == key
            ohf[h] = jnp.where(hit, 1.0, 0.0).astype(BF16)

    def early(w, carry):
        @pl.when(w == 0)
        def _():
            forward(1)
            q_send(xplus(NX - 1), 0, 0, q_right).wait_recv()
            q_send(xplus(NX - 1), 0, 4, q_right).start()
            q_send(xplus(1), 1, 3, q_left).wait_recv()
            q_send(xplus(1), 1, 5, q_left).start()
            for n in range(1, NZ):
                table_z(n).wait_recv()
            arrange(1)

        @pl.when(w == 1)
        def _():
            forward(2)
            arrange(2)

        @pl.when(w == 2)
        def _():
            q_send(xplus(NX - 1), 1, 1, q_right).wait_recv()
            q_send(xplus(1), 0, 2, q_left).wait_recv()
            split_queries(xplus(1))
            split_queries(xplus(NX - 1))

        @pl.when(w == 5)
        def _():
            forward(3)
            arrange(3)

        @pl.when(w == 6)
        def _():
            q_send(xplus(2), 0, 4, q_right).wait_recv()
            q_send(xplus(2), 1, 5, q_left).wait_recv()
            split_queries(xplus(2))

        turn = lax.div(w, 2)
        n = jnp.where(turn == 2, 3, jnp.where(turn == 3, 2, turn))
        attend(xplus(n), lax.rem(w, 2), 0, 3)
        return carry

    lax.fori_loop(0, 2 * NX, early, 0)

    def middle(t, carry):
        group = 1 - lax.rem(t, 2)

        def one(i, inner):
            @pl.when(i == 2)
            def _():
                forward(t + 1)
                arrange(t + 1)

            attend(NX - 1 - i, group, t - group, 2)
            return inner

        lax.fori_loop(0, NX, one, 0)
        return carry

    lax.fori_loop(3, TILES - 2, middle, 0)
    forward(TILES - 1)
    arrange(TILES - 1)

    def late(i, carry):
        owner = lax.rem(i + 1, NX)
        attend(owner, 0, TILES - 1, 1)
        attend(owner, 1, TILES - 3, 3)
        finish(owner)
        return carry

    lax.fori_loop(0, NX, late, 0)

    destinations()

    def rows_of(row):
        return jnp.sum(jnp.where(eye, row, 0.0), axis=1, keepdims=True)

    def spread(n, owner):
        zd = zplus(n)
        return remote(fin.at[owner, zd], gath.at[z, owner], a2a_s.at[owner, n], a2a_r.at[owner, n], (x, zd))

    for owner in (1, 2, 3, 0):
        sources = [s for s in range(NX) if min(s, NX - 1 - s) <= owner]
        for n in range(1, NX):
            @pl.when(takes_part(xplus(NX - n), owner))
            def _():
                for copy in ret(n, owner):
                    copy.wait_recv()
        logs = [
            jnp.concatenate([rows_of(gotl[s, owner, j]) for j in range(2)], 0) for s in sources
        ]
        most = logs[0]
        for value in logs[1:]:
            most = jnp.maximum(most, value)
        total = jnp.zeros((CHUNK, HD), F32)
        weight = jnp.zeros((CHUNK, 1), F32)
        for s, value in zip(sources, logs):
            share = jnp.exp2(value - most)
            weight = weight + share
            total = total + share * got[s, owner].astype(F32)
        fin[owner] = (total / weight).astype(BF16).reshape(NZ, CHUNK // NZ, HD)
        for n in range(1, NZ):
            spread(n, owner).start()
        gath[z, owner] = fin[owner, z]

    for owner in range(NX - 1, -1, -1):
        for n in range(1, NZ):
            spread(n, owner).wait_recv()
    arrived = gath[...].reshape(QROWS, HD)
    for h in range(HEADS):
        out_ref[:, h * HD:(h + 1) * HD] = jnp.dot(
            ohf[h], arrived, preferred_element_type=F32
        ).astype(BF16)

    swap.wait_send()
    for copy in own_pass(0, 1) + own_pass(1, 2):
        copy.wait_send()
    for t in range(1, 6):
        pass_right(t, t + 2).wait_send()
    for t in (1, 2, 3, 4, 6):
        pass_left(t, min(t + 2, TILES - 1)).wait_send()
    for copy in q_copies:
        copy.wait_send()
    q_send(xplus(NX - 1), 0, 4, q_right).wait_send()
    q_send(xplus(1), 1, 5, q_left).wait_send()
    for n in range(1, NX):
        table_x(n).wait_send()
        for owner in range(NX):
            @pl.when(takes_part(x, owner))
            def _():
                for copy in ret(n, owner):
                    copy.wait_send()
    for n in range(1, NZ):
        table_z(n).wait_send()
        for owner in range(NX):
            spread(n, owner).wait_send()


def per_device(queries, query_pos, k_cache, v_cache, kept_index, kept_count, route):
    dma = pltpu.SemaphoreType.DMA
    vmem = pltpu.VMEM
    anywhere = pl.BlockSpec(memory_space=pl.ANY)
    return pl.pallas_call(
        kernel,
        out_shape=pltpu.VMEM((ROWS, QROWS), BF16),
        in_specs=[anywhere] * 6 + [pl.BlockSpec(memory_space=pltpu.SMEM)],
        out_specs=pl.BlockSpec(memory_space=vmem),
        scratch_shapes=[
            vmem((LOCAL, 2 * HD), BF16),
            vmem((SLOTS, LOCAL), BF16),
            vmem((4, 128), I32),
            vmem((1, 128), I32),
            vmem((1, 128), I32),
            vmem((ROWS, QROWS), BF16),
            vmem((HALF, 2 * HD), BF16),
            vmem((TILES, 2, HALF, 2 * HD), BF16),
            vmem((2, TILES, 2 * HD, HALF), BF16),
            vmem((2, TILES * HALF, 2 * HD), BF16),
            vmem((2 * HD, SLOTS), BF16),
            vmem((SLOTS, 2 * HD), BF16),
            vmem((NX, NX, CHUNK, HD), BF16),
            vmem((NX, NX, CHUNK, 2 * HD), BF16),
            vmem((NX, NX, CHUNK, 2 * HD), F32),
            vmem((NX, NX, CHUNK, HD), F32),
            vmem((NX, NX, CHUNK, HD), BF16),
            vmem((NX, NX, 2, 1, 128), F32),
            vmem((NX, NX, CHUNK, HD), BF16),
            vmem((NX, NX, 2, 1, 128), F32),
            vmem((NX, NZ, CHUNK // NZ, HD), BF16),
            vmem((NZ, NX, CHUNK // NZ, HD), BF16),
            vmem((NZ, NX, 1, 128), I32),
            vmem((NZ * NX, 128), F32),
            vmem((HEADS, ROWS, QROWS), BF16),
            dma((4, 2)), dma((4,)), dma, dma,
            dma((TILES, 2)), dma((TILES, 2)),
            dma((6,)), dma((6,)),
            dma((NX, NX)), dma((NX, NX)), dma((NX, NX)), dma((NX, NX)),
            dma((NX, NZ)), dma((NX, NZ)),
            dma((NX,)), dma((NX,)),
            dma((NZ,)), dma((NZ,)),
        ],
        compiler_params=pltpu.CompilerParams(
            collective_id=0, has_side_effects=True, vmem_limit_bytes=56 * 1024 * 1024
        ),
    )(
        kept_index.reshape(4, 128), route.reshape(1, 128), query_pos.reshape(1, 128),
        queries, k_cache, v_cache, kept_count,
    )


def solution(mesh):
    placed = (
        P("context", "mp"),
        P("context"),
        P("context", "mp"),
        P("context", "mp"),
        P("context"),
        P("context"),
        P("context"),
    )
    return jax.shard_map(
        per_device, mesh=mesh, in_specs=placed, out_specs=P("context", "mp"), check_vma=False
    )
```

```python
import math

import jax
import jax.numpy as jnp
from jax import lax
from jax.experimental import pallas as pl
from jax.experimental.pallas import tpu as pltpu
from jax.sharding import PartitionSpec as P

MESH = pl.DeviceIdType.MESH
F32, BF16, I32 = jnp.float32, jnp.bfloat16, jnp.int32

HD = 128
NX = 4
NZ = 8
ROWS = 128
HEADS = 8
SLOTS = 512
HALF = SLOTS // 2
LOCAL = 4096
QROWS = ROWS * HEADS
CHUNK = QROWS // NX
TILES = 8
FAR = 1 << 29
LOW = -1e30
HIDDEN = -2e30
QSCALE = math.log2(math.e) / math.sqrt(HD)


def iota(shape, axis):
    return lax.broadcasted_iota(I32, shape, axis)


def kernel(
    idx_hbm, route_hbm, qpos_hbm, q_hbm, k_hbm, v_hbm, count_ref, out_ref,
    cache, hot, idx_ref, route_ref, qpos_ref, q_ref,
    spare, ring, kk, vv, kkd, vvd, qraw, qp, acc, peak, part, partl, got, gotl, fin, gath,
    table, slots, ohf,
    load_sem, small_sem, swap_s, swap_r, ring_s, ring_r, q_s, q_r, ret_s, ret_r, retl_s, retl_r,
    a2a_s, a2a_r, tx_s, tx_r, tz_s, tz_r,
):
    c = lax.axis_index("context")
    x = lax.div(c, NZ)
    z = lax.rem(c, NZ)
    mirror = NX - 1 - x
    right, left = (x, lax.rem(z + 1, NZ)), (x, lax.rem(z + NZ - 1, NZ))

    def at(where):
        return {"context": where[0] * NZ + where[1]}

    def xplus(n):
        return lax.rem(x + n, NX)

    def zplus(n):
        return lax.rem(z + n, NZ)

    def remote(src, dst, send, recv, to):
        return pltpu.make_async_remote_copy(
            src_ref=src, dst_ref=dst, send_sem=send, recv_sem=recv, device_id=at(to), device_id_type=MESH
        )

    smalls = []
    for i, (src, dst) in enumerate(
        ((idx_hbm, idx_ref), (route_hbm, route_ref), (qpos_hbm, qpos_ref), (q_hbm, q_ref))
    ):
        copy = pltpu.make_async_copy(src, dst, small_sem.at[i])
        copy.start()
        smalls.append(copy)
    loads = []
    for i in range(4):
        rows = pl.ds(i * 1024, 1024)
        for side, ref in enumerate((k_hbm, v_hbm)):
            copy = pltpu.make_async_copy(
                ref.at[rows], cache.at[rows, pl.ds(side * HD, HD)], load_sem.at[i, side]
            )
            copy.start()
            loads.append(copy)

    barrier = pltpu.get_barrier_semaphore()
    for n in range(1, NX):
        pl.semaphore_signal(barrier, inc=1, device_id=at((xplus(n), z)), device_id_type=MESH)
    for n in range(1, NZ):
        pl.semaphore_signal(barrier, inc=1, device_id=at((x, zplus(n))), device_id_type=MESH)

    count = count_ref[0]
    eye = iota((128, 128), 0) == iota((128, 128), 1)
    lane = iota((1, 128), 1)

    def column(row):
        return jnp.sum(jnp.where(eye, row.astype(F32), 0.0), axis=1, keepdims=True).astype(I32)

    for copy in smalls[:3]:
        copy.wait()
    kept = idx_ref[...]
    repeat = jnp.broadcast_to(kept[0:1, 0:1], (1, 128))
    for i in (2, 3, 0, 1):
        index = column(jnp.where(lane + 128 * i < count, kept[i:i + 1], repeat))
        for j in range(4):
            hit = iota((128, 1024), 1) == index - 1024 * j
            hot[i * 128:(i + 1) * 128, j * 1024:(j + 1) * 1024] = jnp.where(hit, 1.0, 0.0).astype(BF16)

    route_lane = route_ref[...]
    dest_lane = lax.div(route_lane, ROWS)
    dest_col = column(dest_lane)
    same = dest_col == dest_lane
    first = iota((128, 128), 0)
    second = iota((128, 128), 1)
    before_lane = jnp.sum(jnp.where(same & (first < second), 1.0, 0.0), axis=0, keepdims=True).astype(I32)
    before_col = jnp.sum(jnp.where(same & (second < first), 1.0, 0.0), axis=1, keepdims=True).astype(I32)
    rank_lane = dest_lane * (ROWS // (NX * NZ)) + before_lane
    rank_col = dest_col * (ROWS // (NX * NZ)) + before_col
    slot_col = column(lax.rem(route_lane, ROWS)).astype(F32)
    slot_row = jnp.sum(jnp.where(rank_col == second, slot_col, 0.0), axis=0, keepdims=True).astype(I32)
    table[z, x] = slot_row + ROWS * count

    def gather(half):
        total = jnp.dot(hot[half * HALF:(half + 1) * HALF, :], cache[...], preferred_element_type=F32)
        live = iota((HALF, HD), 0) + HALF * half < count
        keys = jnp.transpose(total[:, :HD].astype(BF16))
        values = jnp.where(live, total[:, HD:], 0.0).astype(BF16)
        return jnp.concatenate([keys, jnp.concatenate([values[:HD], values[HD:]], 1)], 0)

    for copy in loads:
        copy.wait()
    spare[...] = gather(1)
    ring[0, 0] = gather(0)
    pl.semaphore_wait(barrier, NX - 1 + NZ - 1)
    swap = remote(spare, ring.at[0, 1], swap_s, swap_r, (mirror, z))
    swap.start()

    def pass_right(source, target):
        return remote(ring.at[source, 0], ring.at[target, 0], ring_s.at[target, 0], ring_r.at[target, 0], right)

    def pass_left(source, target):
        return remote(ring.at[source, 1], ring.at[target, 1], ring_s.at[target, 1], ring_r.at[target, 1], left)

    def own_pass(half, target):
        return (
            remote(ring.at[0, half], ring.at[target, 0], ring_s.at[target, 0], ring_r.at[target, 0], right),
            remote(ring.at[0, half], ring.at[target, 1], ring_s.at[target, 1], ring_r.at[target, 1], left),
        )

    for copy in own_pass(0, 1):
        copy.start()

    def table_x(n):
        return remote(table.at[z, x], table.at[z, x], tx_s.at[n], tx_r.at[n], (xplus(n), z))

    for n in range(1, NX):
        table_x(n).start()

    smalls[3].wait()
    stacked = jnp.concatenate([q_ref[:, h * HD:(h + 1) * HD] for h in range(HEADS)], 0)
    rank_key = jnp.concatenate([rank_lane + ROWS * h for h in range(HEADS)], 1)
    within = iota((CHUNK, 1), 0)
    place = lax.div(within, 32) * 4 + lax.rem(within, 4)
    head_of = lax.rem(lax.div(within, 4), HEADS)
    for i in range(NX):
        hit = rank_key == place + 32 * i + ROWS * head_of
        one = jnp.where(hit, 1.0, 0.0).astype(BF16)
        qraw[x, i] = jnp.dot(one, stacked, preferred_element_type=F32).astype(BF16)

    q_right, q_left = (xplus(1), z), (xplus(NX - 1), z)

    def q_send(owner, half, number, to):
        view = qraw.at[owner, pl.ds(2 * half, 2)]
        return remote(view, view, q_s.at[number], q_r.at[number], to)

    q_copies = [
        q_send(x, 0, 0, q_right), q_send(x, 1, 3, q_left),
        q_send(x, 1, 1, q_right), q_send(x, 0, 2, q_left),
    ]
    for copy in q_copies:
        copy.start()

    def split_queries(owner):
        for i in range(NX):
            scaled = qraw[owner, i].astype(F32) * QSCALE
            high = scaled.astype(BF16)
            low = (scaled - high.astype(F32)).astype(BF16)
            qp[owner, i] = jnp.concatenate([high, low], 1)

    split_queries(x)
    for n in range(1, NX):
        acc[xplus(n)] = jnp.zeros((NX, CHUNK, 2 * HD), F32)
        peak[xplus(n)] = jnp.full((NX, CHUNK, HD), LOW, F32)

    def keys_of(block):
        return jnp.concatenate([block[:HD], block[:HD]], 0)

    def values_of(block, live):
        mark = jnp.where(live, 1.0, 0.0).astype(BF16)
        return jnp.concatenate([jnp.concatenate([block[HD:, :HD], block[HD:, HD:]], 0), mark], 1)

    slot_wide = iota((HALF, HD), 0)
    for half, block in enumerate((ring[0, 0], spare[...])):
        kkd[:, half * HALF:(half + 1) * HALF] = keys_of(block)
        vvd[half * HALF:(half + 1) * HALF] = values_of(block, slot_wide + HALF * half < count)
    key_pos = jnp.concatenate(
        [jnp.where(lane + 128 * i < count, kept[i:i + 1], FAR) for i in range(4)], 1
    )
    local_pos = (qpos_ref[...] - c * LOCAL).astype(F32)
    scores = [jnp.dot(qp[x, i], kkd[...], preferred_element_type=F32) for i in range(NX)]
    for i in range(NX):
        own_pos = jnp.sum(
            jnp.where(rank_lane == place + 32 * i, local_pos, 0.0), axis=1, keepdims=True
        ).astype(I32)
        seen_scores = jnp.where(key_pos <= own_pos, scores[i], HIDDEN)
        new_peak = jnp.broadcast_to(
            jnp.maximum(jnp.max(seen_scores, axis=1, keepdims=True), LOW), (CHUNK, HD)
        )
        weights = jnp.exp2(seen_scores - jnp.concatenate([new_peak] * 4, 1)).astype(BF16)
        acc[x, i] = jnp.dot(weights, vvd[...], preferred_element_type=F32)
        peak[x, i] = new_peak

    for n in range(1, NX):
        table_x(n).wait_recv()

    def table_z(n):
        return remote(table.at[z], table.at[z], tz_s.at[n], tz_r.at[n], (x, zplus(n)))

    for n in range(1, NZ):
        table_z(n).start()

    swap.wait_recv()
    for copy in own_pass(1, 2):
        copy.start()

    def owner_row(group):
        return jnp.where(group == 0, x, mirror)

    def origin_of(h):
        step = lax.div(h + 1, 2)
        return lax.rem(jnp.where(lax.rem(h, 2) == 1, z + NZ - step, z + step), NZ)

    def prepare(t, side, group, h):
        block = ring[t, side]
        live_count = lax.div(table[origin_of(h), owner_row(group)], ROWS)
        kk[group, h] = keys_of(block)
        vv[group, pl.ds(h * HALF, HALF)] = values_of(block, slot_wide + HALF * group < live_count)

    def forward(t):
        pass_right(t, t).wait_recv()
        pass_left(t, t).wait_recv()

        @pl.when(t <= 5)
        def _():
            pass_right(t, t + 2).start()

        @pl.when((t <= 4) | (t == 6))
        def _():
            pass_left(t, jnp.minimum(t + 2, TILES - 1)).start()

    def arrange(t):
        end = t == TILES - 1
        group = 1 - lax.rem(t, 2)
        h = t - group
        prepare(t, 0, group, h)
        prepare(t, 1, jnp.where(end, 1, group), jnp.where(end, h, h + 1))

    def attend(owner, group, start, number):
        halves = [start + k for k in range(number)]
        row = owner_row(group)
        every = owner > row
        visible = [origin_of(h) < z for h in halves]
        some = visible[0]
        for v in visible[1:]:
            some = some | v

        def update(bias):
            scores = []
            for i in range(NX):
                parts = [jnp.dot(qp[owner, i], kk[group, h], preferred_element_type=F32) for h in halves]
                if bias is not None:
                    parts = [p + b for p, b in zip(parts, bias)]
                scores.append(parts)
            for i in range(NX):
                old_peak = peak[owner, i]
                top = scores[i][0]
                for p in scores[i][1:]:
                    top = jnp.maximum(top, p)
                new_peak = jnp.maximum(jnp.max(top, axis=1, keepdims=True), old_peak)
                twice = jnp.concatenate([new_peak, new_peak], 1)
                weights = jnp.concatenate([jnp.exp2(p - twice).astype(BF16) for p in scores[i]], 1)
                summed = jnp.dot(
                    weights, vv[group, pl.ds(start * HALF, number * HALF)], preferred_element_type=F32
                )
                scale = jnp.exp2(old_peak - new_peak)
                acc[owner, i] = acc[owner, i] * jnp.concatenate([scale, scale], 1) + summed
                peak[owner, i] = new_peak

        @pl.when(every)
        def _():
            update(None)

        @pl.when((owner == row) & some)
        def _():
            update([jnp.where(v, 0.0, HIDDEN) for v in visible])

    def takes_part(source, owner):
        return jnp.minimum(source, NX - 1 - source) <= owner

    def ret(n, owner):
        xd = xplus(n)
        return (
            remote(part.at[owner, xd], got.at[x, owner], ret_s.at[n, owner], ret_r.at[n, owner], (xd, z)),
            remote(partl.at[xd, owner], gotl.at[x, owner], retl_s.at[n, owner], retl_r.at[n, owner], (xd, z)),
        )

    def finish(owner):
        for i in range(NX):
            top = acc[owner, i][:, :HD]
            bottom = acc[owner, i][:, HD:]
            alive = bottom > 0.0
            safe = jnp.where(alive, bottom, 1.0)
            part[owner, i] = (top / safe).astype(BF16)
            logs = jnp.where(alive, peak[owner, i] + jnp.log(safe) * math.log2(math.e), LOW)
            for j in range(2):
                partl[i, owner, j] = jnp.sum(
                    jnp.where(eye, logs[j * 128:(j + 1) * 128], 0.0), axis=0, keepdims=True
                )

        @pl.when(takes_part(x, owner))
        def _():
            for n in range(1, NX):
                for copy in ret(n, owner):
                    copy.start()

        got[x, owner] = part[owner, x]
        gotl[x, owner] = partl[x, owner]

    prepare(0, 0, 0, 0)
    prepare(0, 1, 1, 0)

    def destinations():
        for zz in range(NZ):
            for xx in range(NX):
                slots[xx * NZ + zz:xx * NZ + zz + 1, :] = lax.rem(table[zz, xx], ROWS).astype(F32)
        wide = iota((128, QROWS), 1)
        pick = jnp.where(iota((128, QROWS), 0) == c * 4 + lax.rem(wide, 4), 1.0, 0.0).astype(BF16)
        picked = jnp.dot(slots[...].astype(BF16), pick, preferred_element_type=F32)
        mine = iota((32, QROWS), 0) == lax.div(iota((32, QROWS), 1), 32)
        slot_of = jnp.sum(jnp.where(mine, picked, 0.0), axis=0, keepdims=True).astype(I32)
        lanes = iota((1, QROWS), 1)
        key = slot_of + ROWS * lax.rem(lax.div(lanes, 4), HEADS)
        for h in range(HEADS):
            hit = iota((ROWS, QROWS), 0) + ROWS * h == key
            ohf[h] = jnp.where(hit, 1.0, 0.0).astype(BF16)

    def early(w, carry):
        @pl.when(w == 0)
        def _():
            forward(1)
            q_send(xplus(NX - 1), 0, 0, q_right).wait_recv()
            q_send(xplus(NX - 1), 0, 4, q_right).start()
            q_send(xplus(1), 1, 3, q_left).wait_recv()
            q_send(xplus(1), 1, 5, q_left).start()
            for n in range(1, NZ):
                table_z(n).wait_recv()
            arrange(1)

        @pl.when(w == 1)
        def _():
            forward(2)
            arrange(2)

        @pl.when(w == 2)
        def _():
            q_send(xplus(NX - 1), 1, 1, q_right).wait_recv()
            q_send(xplus(1), 0, 2, q_left).wait_recv()
            split_queries(xplus(1))
            split_queries(xplus(NX - 1))

        @pl.when(w == 5)
        def _():
            forward(3)
            arrange(3)

        @pl.when(w == 6)
        def _():
            q_send(xplus(2), 0, 4, q_right).wait_recv()
            q_send(xplus(2), 1, 5, q_left).wait_recv()
            split_queries(xplus(2))

        turn = lax.div(w, 2)
        n = jnp.where(turn == 2, 3, jnp.where(turn == 3, 2, turn))
        attend(xplus(n), lax.rem(w, 2), 0, 3)
        return carry

    lax.fori_loop(0, 2 * NX, early, 0)

    def middle(t, carry):
        group = 1 - lax.rem(t, 2)

        def one(i, inner):
            @pl.when(i == 2)
            def _():
                forward(t + 1)
                arrange(t + 1)

            attend(NX - 1 - i, group, t - group, 2)
            return inner

        lax.fori_loop(0, NX, one, 0)
        return carry

    lax.fori_loop(3, TILES - 2, middle, 0)
    forward(TILES - 1)
    arrange(TILES - 1)

    def late(i, carry):
        owner = lax.rem(i + 1, NX)
        attend(owner, 0, TILES - 1, 1)
        attend(owner, 1, TILES - 3, 3)
        finish(owner)
        return carry

    lax.fori_loop(0, NX, late, 0)

    destinations()

    def rows_of(row):
        return jnp.sum(jnp.where(eye, row, 0.0), axis=1, keepdims=True)

    def spread(n, owner):
        zd = zplus(n)
        return remote(fin.at[owner, zd], gath.at[owner, z], a2a_s.at[owner, n], a2a_r.at[owner, n], (x, zd))

    for owner in (1, 2, 3, 0):
        sources = [s for s in range(NX) if min(s, NX - 1 - s) <= owner]
        for n in range(1, NX):
            @pl.when(takes_part(xplus(NX - n), owner))
            def _():
                for copy in ret(n, owner):
                    copy.wait_recv()
        logs = [
            jnp.concatenate([rows_of(gotl[s, owner, j]) for j in range(2)], 0) for s in sources
        ]
        most = logs[0]
        for value in logs[1:]:
            most = jnp.maximum(most, value)
        total = jnp.zeros((CHUNK, HD), F32)
        weight = jnp.zeros((CHUNK, 1), F32)
        for s, value in zip(sources, logs):
            share = jnp.exp2(value - most)
            weight = weight + share
            total = total + share * got[s, owner].astype(F32)
        fin[owner] = (total / weight).astype(BF16).reshape(NZ, CHUNK // NZ, HD)
        for n in range(1, NZ):
            spread(n, owner).start()
        gath[owner, z] = fin[owner, z]

    placed = [None] * HEADS
    for owner in (1, 2, 3, 0):
        for n in range(1, NZ):
            spread(n, owner).wait_recv()
        arrived = gath[owner].reshape(CHUNK, HD)
        for h in range(HEADS):
            share = jnp.dot(
                ohf[h, :, owner * CHUNK:(owner + 1) * CHUNK], arrived, preferred_element_type=F32
            )
            placed[h] = share if placed[h] is None else placed[h] + share
    for h in range(HEADS):
        out_ref[:, h * HD:(h + 1) * HD] = placed[h].astype(BF16)

    swap.wait_send()
    for copy in own_pass(0, 1) + own_pass(1, 2):
        copy.wait_send()
    for t in range(1, 6):
        pass_right(t, t + 2).wait_send()
    for t in (1, 2, 3, 4, 6):
        pass_left(t, min(t + 2, TILES - 1)).wait_send()
    for copy in q_copies:
        copy.wait_send()
    q_send(xplus(NX - 1), 0, 4, q_right).wait_send()
    q_send(xplus(1), 1, 5, q_left).wait_send()
    for n in range(1, NX):
        table_x(n).wait_send()
        for owner in range(NX):
            @pl.when(takes_part(x, owner))
            def _():
                for copy in ret(n, owner):
                    copy.wait_send()
    for n in range(1, NZ):
        table_z(n).wait_send()
        for owner in range(NX):
            spread(n, owner).wait_send()


def per_device(queries, query_pos, k_cache, v_cache, kept_index, kept_count, route):
    dma = pltpu.SemaphoreType.DMA
    vmem = pltpu.VMEM
    anywhere = pl.BlockSpec(memory_space=pl.ANY)
    return pl.pallas_call(
        kernel,
        out_shape=pltpu.VMEM((ROWS, QROWS), BF16),
        in_specs=[anywhere] * 6 + [pl.BlockSpec(memory_space=pltpu.SMEM)],
        out_specs=pl.BlockSpec(memory_space=vmem),
        scratch_shapes=[
            vmem((LOCAL, 2 * HD), BF16),
            vmem((SLOTS, LOCAL), BF16),
            vmem((4, 128), I32),
            vmem((1, 128), I32),
            vmem((1, 128), I32),
            vmem((ROWS, QROWS), BF16),
            vmem((HALF, 2 * HD), BF16),
            vmem((TILES, 2, HALF, 2 * HD), BF16),
            vmem((2, TILES, 2 * HD, HALF), BF16),
            vmem((2, TILES * HALF, 2 * HD), BF16),
            vmem((2 * HD, SLOTS), BF16),
            vmem((SLOTS, 2 * HD), BF16),
            vmem((NX, NX, CHUNK, HD), BF16),
            vmem((NX, NX, CHUNK, 2 * HD), BF16),
            vmem((NX, NX, CHUNK, 2 * HD), F32),
            vmem((NX, NX, CHUNK, HD), F32),
            vmem((NX, NX, CHUNK, HD), BF16),
            vmem((NX, NX, 2, 1, 128), F32),
            vmem((NX, NX, CHUNK, HD), BF16),
            vmem((NX, NX, 2, 1, 128), F32),
            vmem((NX, NZ, CHUNK // NZ, HD), BF16),
            vmem((NX, NZ, CHUNK // NZ, HD), BF16),
            vmem((NZ, NX, 1, 128), I32),
            vmem((NZ * NX, 128), F32),
            vmem((HEADS, ROWS, QROWS), BF16),
            dma((4, 2)), dma((4,)), dma, dma,
            dma((TILES, 2)), dma((TILES, 2)),
            dma((6,)), dma((6,)),
            dma((NX, NX)), dma((NX, NX)), dma((NX, NX)), dma((NX, NX)),
            dma((NX, NZ)), dma((NX, NZ)),
            dma((NX,)), dma((NX,)),
            dma((NZ,)), dma((NZ,)),
        ],
        compiler_params=pltpu.CompilerParams(
            collective_id=0, has_side_effects=True, vmem_limit_bytes=56 * 1024 * 1024
        ),
    )(
        kept_index.reshape(4, 128), route.reshape(1, 128), query_pos.reshape(1, 128),
        queries, k_cache, v_cache, kept_count,
    )


def solution(mesh):
    placed = (
        P("context", "mp"),
        P("context"),
        P("context", "mp"),
        P("context", "mp"),
        P("context"),
        P("context"),
        P("context"),
    )
    return jax.shard_map(
        per_device, mesh=mesh, in_specs=placed, out_specs=P("context", "mp"), check_vma=False
    )
```

```python
import math

import jax
import jax.numpy as jnp
from jax import lax
from jax.experimental import pallas as pl
from jax.experimental.pallas import tpu as pltpu
from jax.sharding import PartitionSpec as P

MESH = pl.DeviceIdType.MESH
F32, BF16, I32 = jnp.float32, jnp.bfloat16, jnp.int32

HD = 128
NX = 4
NZ = 8
ROWS = 128
HEADS = 8
SLOTS = 512
HALF = SLOTS // 2
LOCAL = 4096
QROWS = ROWS * HEADS
CHUNK = QROWS // NX
TILES = 8
FAR = 1 << 29
LOW = -1e30
HIDDEN = -2e30
QSCALE = math.log2(math.e) / math.sqrt(HD)


def iota(shape, axis):
    return lax.broadcasted_iota(I32, shape, axis)


def kernel(
    idx_hbm, route_hbm, qpos_hbm, q_hbm, k_hbm, v_hbm, count_ref, out_ref,
    cache, hot, idx_ref, route_ref, qpos_ref, q_ref,
    spare, ring, kk, vv, kkd, vvd, qraw, qp, acc, peak, part, partl, got, gotl, fin, gath,
    table, slots, ohf,
    load_sem, small_sem, swap_s, swap_r, ring_s, ring_r, q_s, q_r, ret_s, ret_r, retl_s, retl_r,
    a2a_s, a2a_r, tx_s, tx_r, tz_s, tz_r,
):
    c = lax.axis_index("context")
    x = lax.div(c, NZ)
    z = lax.rem(c, NZ)
    mirror = NX - 1 - x
    right, left = (x, lax.rem(z + 1, NZ)), (x, lax.rem(z + NZ - 1, NZ))

    def at(where):
        return {"context": where[0] * NZ + where[1]}

    def xplus(n):
        return lax.rem(x + n, NX)

    def zplus(n):
        return lax.rem(z + n, NZ)

    def remote(src, dst, send, recv, to):
        return pltpu.make_async_remote_copy(
            src_ref=src, dst_ref=dst, send_sem=send, recv_sem=recv, device_id=at(to), device_id_type=MESH
        )

    smalls = []
    for i, (src, dst) in enumerate(
        ((idx_hbm, idx_ref), (route_hbm, route_ref), (qpos_hbm, qpos_ref), (q_hbm, q_ref))
    ):
        copy = pltpu.make_async_copy(src, dst, small_sem.at[i])
        copy.start()
        smalls.append(copy)
    loads = []
    for i in range(4):
        rows = pl.ds(i * 1024, 1024)
        for side, ref in enumerate((k_hbm, v_hbm)):
            copy = pltpu.make_async_copy(
                ref.at[rows], cache.at[rows, pl.ds(side * HD, HD)], load_sem.at[i, side]
            )
            copy.start()
            loads.append(copy)

    barrier = pltpu.get_barrier_semaphore()
    for n in range(1, NX):
        pl.semaphore_signal(barrier, inc=1, device_id=at((xplus(n), z)), device_id_type=MESH)
    for n in range(1, NZ):
        pl.semaphore_signal(barrier, inc=1, device_id=at((x, zplus(n))), device_id_type=MESH)

    count = count_ref[0]
    eye = iota((128, 128), 0) == iota((128, 128), 1)
    lane = iota((1, 128), 1)

    def column(row):
        return jnp.sum(jnp.where(eye, row.astype(F32), 0.0), axis=1, keepdims=True).astype(I32)

    for copy in smalls[:3]:
        copy.wait()
    kept = idx_ref[...]
    repeat = jnp.broadcast_to(kept[0:1, 0:1], (1, 128))
    for i in (2, 3, 0, 1):
        index = column(jnp.where(lane + 128 * i < count, kept[i:i + 1], repeat))
        for j in range(4):
            hit = iota((128, 1024), 1) == index - 1024 * j
            hot[i * 128:(i + 1) * 128, j * 1024:(j + 1) * 1024] = jnp.where(hit, 1.0, 0.0).astype(BF16)

    route_lane = route_ref[...]
    dest_lane = lax.div(route_lane, ROWS)
    dest_col = column(dest_lane)
    same = dest_col == dest_lane
    first = iota((128, 128), 0)
    second = iota((128, 128), 1)
    before_lane = jnp.sum(jnp.where(same & (first < second), 1.0, 0.0), axis=0, keepdims=True).astype(I32)
    before_col = jnp.sum(jnp.where(same & (second < first), 1.0, 0.0), axis=1, keepdims=True).astype(I32)
    rank_lane = dest_lane * (ROWS // (NX * NZ)) + before_lane
    rank_col = dest_col * (ROWS // (NX * NZ)) + before_col
    slot_col = column(lax.rem(route_lane, ROWS)).astype(F32)
    slot_row = jnp.sum(jnp.where(rank_col == second, slot_col, 0.0), axis=0, keepdims=True).astype(I32)
    table[z, x] = slot_row + ROWS * count

    def gather(half):
        total = jnp.dot(hot[half * HALF:(half + 1) * HALF, :], cache[...], preferred_element_type=F32)
        live = iota((HALF, HD), 0) + HALF * half < count
        keys = jnp.transpose(total[:, :HD].astype(BF16))
        values = jnp.where(live, total[:, HD:], 0.0).astype(BF16)
        return jnp.concatenate([keys, jnp.concatenate([values[:HD], values[HD:]], 1)], 0)

    for copy in loads:
        copy.wait()
    spare[...] = gather(1)
    ring[0, 0] = gather(0)
    pl.semaphore_wait(barrier, NX - 1 + NZ - 1)
    swap = remote(spare, ring.at[0, 1], swap_s, swap_r, (mirror, z))
    swap.start()

    def pass_right(source, target):
        return remote(ring.at[source, 0], ring.at[target, 0], ring_s.at[target, 0], ring_r.at[target, 0], right)

    def pass_left(source, target):
        return remote(ring.at[source, 1], ring.at[target, 1], ring_s.at[target, 1], ring_r.at[target, 1], left)

    def own_pass(half, target):
        return (
            remote(ring.at[0, half], ring.at[target, 0], ring_s.at[target, 0], ring_r.at[target, 0], right),
            remote(ring.at[0, half], ring.at[target, 1], ring_s.at[target, 1], ring_r.at[target, 1], left),
        )

    for copy in own_pass(0, 1):
        copy.start()

    def table_x(n):
        return remote(table.at[z, x], table.at[z, x], tx_s.at[n], tx_r.at[n], (xplus(n), z))

    for n in range(1, NX):
        table_x(n).start()

    smalls[3].wait()
    stacked = jnp.concatenate([q_ref[:, h * HD:(h + 1) * HD] for h in range(HEADS)], 0)
    rank_key = jnp.concatenate([rank_lane + ROWS * h for h in range(HEADS)], 1)
    within = iota((CHUNK, 1), 0)
    place = lax.div(within, 32) * 4 + lax.rem(within, 4)
    head_of = lax.rem(lax.div(within, 4), HEADS)
    for i in range(NX):
        hit = rank_key == place + 32 * i + ROWS * head_of
        one = jnp.where(hit, 1.0, 0.0).astype(BF16)
        qraw[x, i] = jnp.dot(one, stacked, preferred_element_type=F32).astype(BF16)

    q_right, q_left = (xplus(1), z), (xplus(NX - 1), z)

    def q_send(owner, half, number, to):
        view = qraw.at[owner, pl.ds(2 * half, 2)]
        return remote(view, view, q_s.at[number], q_r.at[number], to)

    q_copies = [
        q_send(x, 0, 0, q_right), q_send(x, 1, 3, q_left),
        q_send(x, 1, 1, q_right), q_send(x, 0, 2, q_left),
    ]
    for copy in q_copies:
        copy.start()

    def split_queries(owner):
        for i in range(NX):
            scaled = qraw[owner, i].astype(F32) * QSCALE
            high = scaled.astype(BF16)
            low = (scaled - high.astype(F32)).astype(BF16)
            qp[owner, i] = jnp.concatenate([high, low], 1)

    split_queries(x)
    for n in range(1, NX):
        acc[xplus(n)] = jnp.zeros((NX, CHUNK, 2 * HD), F32)
        peak[xplus(n)] = jnp.full((NX, CHUNK, HD), LOW, F32)

    def keys_of(block):
        return jnp.concatenate([block[:HD], block[:HD]], 0)

    def values_of(block, live):
        mark = jnp.where(live, 1.0, 0.0).astype(BF16)
        return jnp.concatenate([jnp.concatenate([block[HD:, :HD], block[HD:, HD:]], 0), mark], 1)

    slot_wide = iota((HALF, HD), 0)
    for half, block in enumerate((ring[0, 0], spare[...])):
        kkd[:, half * HALF:(half + 1) * HALF] = keys_of(block)
        vvd[half * HALF:(half + 1) * HALF] = values_of(block, slot_wide + HALF * half < count)
    key_pos = jnp.concatenate(
        [jnp.where(lane + 128 * i < count, kept[i:i + 1], FAR) for i in range(4)], 1
    )
    local_pos = (qpos_ref[...] - c * LOCAL).astype(F32)
    scores = [jnp.dot(qp[x, i], kkd[...], preferred_element_type=F32) for i in range(NX)]
    for i in range(NX):
        own_pos = jnp.sum(
            jnp.where(rank_lane == place + 32 * i, local_pos, 0.0), axis=1, keepdims=True
        ).astype(I32)
        seen_scores = jnp.where(key_pos <= own_pos, scores[i], HIDDEN)
        new_peak = jnp.broadcast_to(
            jnp.maximum(jnp.max(seen_scores, axis=1, keepdims=True), LOW), (CHUNK, HD)
        )
        weights = jnp.exp2(seen_scores - jnp.concatenate([new_peak] * 4, 1)).astype(BF16)
        acc[x, i] = jnp.dot(weights, vvd[...], preferred_element_type=F32)
        peak[x, i] = new_peak

    for n in range(1, NX):
        table_x(n).wait_recv()

    def table_z(n):
        return remote(table.at[z], table.at[z], tz_s.at[n], tz_r.at[n], (x, zplus(n)))

    for n in range(1, NZ):
        table_z(n).start()

    swap.wait_recv()
    for copy in own_pass(1, 2):
        copy.start()

    def owner_row(group):
        return jnp.where(group == 0, x, mirror)

    def origin_of(h):
        step = lax.div(h + 1, 2)
        return lax.rem(jnp.where(lax.rem(h, 2) == 1, z + NZ - step, z + step), NZ)

    def prepare(t, side, group, h):
        block = ring[t, side]
        live_count = lax.div(table[origin_of(h), owner_row(group)], ROWS)
        kk[group, h] = keys_of(block)
        vv[group, pl.ds(h * HALF, HALF)] = values_of(block, slot_wide + HALF * group < live_count)

    def forward(t):
        pass_right(t, t).wait_recv()
        pass_left(t, t).wait_recv()

        @pl.when(t <= 5)
        def _():
            pass_right(t, t + 2).start()

        @pl.when((t <= 4) | (t == 6))
        def _():
            pass_left(t, jnp.minimum(t + 2, TILES - 1)).start()

    def arrange(t):
        end = t == TILES - 1
        group = 1 - lax.rem(t, 2)
        h = t - group
        prepare(t, 0, group, h)
        prepare(t, 1, jnp.where(end, 1, group), jnp.where(end, h, h + 1))

    def attend(owner, group, start, number):
        halves = [start + k for k in range(number)]
        row = owner_row(group)
        every = owner > row
        visible = [origin_of(h) < z for h in halves]
        some = visible[0]
        for v in visible[1:]:
            some = some | v

        def update(bias):
            scores = []
            for i in range(NX):
                parts = [jnp.dot(qp[owner, i], kk[group, h], preferred_element_type=F32) for h in halves]
                if bias is not None:
                    parts = [p + b for p, b in zip(parts, bias)]
                scores.append(parts)
            for i in range(NX):
                old_peak = peak[owner, i]
                top = scores[i][0]
                for p in scores[i][1:]:
                    top = jnp.maximum(top, p)
                new_peak = jnp.maximum(jnp.max(top, axis=1, keepdims=True), old_peak)
                twice = jnp.concatenate([new_peak, new_peak], 1)
                weights = jnp.concatenate([jnp.exp2(p - twice).astype(BF16) for p in scores[i]], 1)
                summed = jnp.dot(
                    weights, vv[group, pl.ds(start * HALF, number * HALF)], preferred_element_type=F32
                )
                scale = jnp.exp2(old_peak - new_peak)
                acc[owner, i] = acc[owner, i] * jnp.concatenate([scale, scale], 1) + summed
                peak[owner, i] = new_peak

        @pl.when(every)
        def _():
            update(None)

        @pl.when((owner == row) & some)
        def _():
            update([jnp.where(v, 0.0, HIDDEN) for v in visible])

    def takes_part(source, owner):
        return jnp.minimum(source, NX - 1 - source) <= owner

    def ret(n, owner):
        xd = xplus(n)
        return (
            remote(part.at[owner, xd], got.at[x, owner], ret_s.at[n, owner], ret_r.at[n, owner], (xd, z)),
            remote(partl.at[xd, owner], gotl.at[x, owner], retl_s.at[n, owner], retl_r.at[n, owner], (xd, z)),
        )

    def finish(owner):
        for i in range(NX):
            top = acc[owner, i][:, :HD]
            bottom = acc[owner, i][:, HD:]
            alive = bottom > 0.0
            safe = jnp.where(alive, bottom, 1.0)
            part[owner, i] = (top / safe).astype(BF16)
            tops = jnp.where(alive, peak[owner, i], LOW)
            for j in range(2):
                rows = slice(j * 128, (j + 1) * 128)
                top_row = jnp.sum(jnp.where(eye, tops[rows], 0.0), axis=0, keepdims=True)
                sum_row = jnp.sum(jnp.where(eye, safe[rows], 0.0), axis=0, keepdims=True)
                partl[i, owner, j] = top_row + jnp.log(sum_row) * math.log2(math.e)

        @pl.when(takes_part(x, owner))
        def _():
            for n in range(1, NX):
                for copy in ret(n, owner):
                    copy.start()

        got[x, owner] = part[owner, x]
        gotl[x, owner] = partl[x, owner]

    prepare(0, 0, 0, 0)
    prepare(0, 1, 1, 0)

    def destinations():
        for zz in range(NZ):
            for xx in range(NX):
                slots[xx * NZ + zz:xx * NZ + zz + 1, :] = lax.rem(table[zz, xx], ROWS).astype(F32)
        wide = iota((128, QROWS), 1)
        pick = jnp.where(iota((128, QROWS), 0) == c * 4 + lax.rem(wide, 4), 1.0, 0.0).astype(BF16)
        picked = jnp.dot(slots[...].astype(BF16), pick, preferred_element_type=F32)
        mine = iota((32, QROWS), 0) == lax.div(iota((32, QROWS), 1), 32)
        slot_of = jnp.sum(jnp.where(mine, picked, 0.0), axis=0, keepdims=True).astype(I32)
        lanes = iota((1, QROWS), 1)
        key = slot_of + ROWS * lax.rem(lax.div(lanes, 4), HEADS)
        for h in range(HEADS):
            hit = iota((ROWS, QROWS), 0) + ROWS * h == key
            ohf[h] = jnp.where(hit, 1.0, 0.0).astype(BF16)

    def early(w, carry):
        @pl.when(w == 0)
        def _():
            forward(1)
            q_send(xplus(NX - 1), 0, 0, q_right).wait_recv()
            q_send(xplus(NX - 1), 0, 4, q_right).start()
            q_send(xplus(1), 1, 3, q_left).wait_recv()
            q_send(xplus(1), 1, 5, q_left).start()
            for n in range(1, NZ):
                table_z(n).wait_recv()
            arrange(1)

        @pl.when(w == 1)
        def _():
            forward(2)
            arrange(2)

        @pl.when(w == 2)
        def _():
            q_send(xplus(NX - 1), 1, 1, q_right).wait_recv()
            q_send(xplus(1), 0, 2, q_left).wait_recv()
            split_queries(xplus(1))
            split_queries(xplus(NX - 1))

        @pl.when(w == 5)
        def _():
            forward(3)
            arrange(3)

        @pl.when(w == 6)
        def _():
            q_send(xplus(2), 0, 4, q_right).wait_recv()
            q_send(xplus(2), 1, 5, q_left).wait_recv()
            split_queries(xplus(2))

        turn = lax.div(w, 2)
        n = jnp.where(turn == 2, 3, jnp.where(turn == 3, 2, turn))
        attend(xplus(n), lax.rem(w, 2), 0, 3)
        return carry

    lax.fori_loop(0, 2 * NX, early, 0)

    def middle(t, carry):
        group = 1 - lax.rem(t, 2)

        def one(i, inner):
            @pl.when(i == 2)
            def _():
                forward(t + 1)
                arrange(t + 1)

            attend(NX - 1 - i, group, t - group, 2)
            return inner

        lax.fori_loop(0, NX, one, 0)
        return carry

    lax.fori_loop(3, TILES - 2, middle, 0)
    forward(TILES - 1)
    arrange(TILES - 1)

    def late(i, carry):
        owner = lax.rem(i + 1, NX)
        attend(owner, 0, TILES - 1, 1)
        attend(owner, 1, TILES - 3, 3)
        finish(owner)
        return carry

    lax.fori_loop(0, NX, late, 0)

    destinations()

    def rows_of(row):
        return jnp.sum(jnp.where(eye, row, 0.0), axis=1, keepdims=True)

    def spread(n, owner):
        zd = zplus(n)
        return remote(fin.at[owner, zd], gath.at[owner, z], a2a_s.at[owner, n], a2a_r.at[owner, n], (x, zd))

    for owner in (1, 2, 3, 0):
        sources = [s for s in range(NX) if min(s, NX - 1 - s) <= owner]
        for n in range(1, NX):
            @pl.when(takes_part(xplus(NX - n), owner))
            def _():
                for copy in ret(n, owner):
                    copy.wait_recv()
        logs = [
            jnp.concatenate([rows_of(gotl[s, owner, j]) for j in range(2)], 0) for s in sources
        ]
        most = logs[0]
        for value in logs[1:]:
            most = jnp.maximum(most, value)
        total = jnp.zeros((CHUNK, HD), F32)
        weight = jnp.zeros((CHUNK, 1), F32)
        for s, value in zip(sources, logs):
            share = jnp.exp2(value - most)
            weight = weight + share
            total = total + share * got[s, owner].astype(F32)
        fin[owner] = (total / weight).astype(BF16).reshape(NZ, CHUNK // NZ, HD)
        for n in range(1, NZ):
            spread(n, owner).start()
        gath[owner, z] = fin[owner, z]

    placed = [None] * HEADS
    for owner in (1, 2, 3, 0):
        for n in range(1, NZ):
            spread(n, owner).wait_recv()
        arrived = gath[owner].reshape(CHUNK, HD)
        for h in range(HEADS):
            share = jnp.dot(
                ohf[h, :, owner * CHUNK:(owner + 1) * CHUNK], arrived, preferred_element_type=F32
            )
            placed[h] = share if placed[h] is None else placed[h] + share
    for h in range(HEADS):
        out_ref[:, h * HD:(h + 1) * HD] = placed[h].astype(BF16)

    swap.wait_send()
    for copy in own_pass(0, 1) + own_pass(1, 2):
        copy.wait_send()
    for t in range(1, 6):
        pass_right(t, t + 2).wait_send()
    for t in (1, 2, 3, 4, 6):
        pass_left(t, min(t + 2, TILES - 1)).wait_send()
    for copy in q_copies:
        copy.wait_send()
    q_send(xplus(NX - 1), 0, 4, q_right).wait_send()
    q_send(xplus(1), 1, 5, q_left).wait_send()
    for n in range(1, NX):
        table_x(n).wait_send()
        for owner in range(NX):
            @pl.when(takes_part(x, owner))
            def _():
                for copy in ret(n, owner):
                    copy.wait_send()
    for n in range(1, NZ):
        table_z(n).wait_send()
        for owner in range(NX):
            spread(n, owner).wait_send()


def per_device(queries, query_pos, k_cache, v_cache, kept_index, kept_count, route):
    dma = pltpu.SemaphoreType.DMA
    vmem = pltpu.VMEM
    anywhere = pl.BlockSpec(memory_space=pl.ANY)
    return pl.pallas_call(
        kernel,
        out_shape=pltpu.VMEM((ROWS, QROWS), BF16),
        in_specs=[anywhere] * 6 + [pl.BlockSpec(memory_space=pltpu.SMEM)],
        out_specs=pl.BlockSpec(memory_space=vmem),
        scratch_shapes=[
            vmem((LOCAL, 2 * HD), BF16),
            vmem((SLOTS, LOCAL), BF16),
            vmem((4, 128), I32),
            vmem((1, 128), I32),
            vmem((1, 128), I32),
            vmem((ROWS, QROWS), BF16),
            vmem((HALF, 2 * HD), BF16),
            vmem((TILES, 2, HALF, 2 * HD), BF16),
            vmem((2, TILES, 2 * HD, HALF), BF16),
            vmem((2, TILES * HALF, 2 * HD), BF16),
            vmem((2 * HD, SLOTS), BF16),
            vmem((SLOTS, 2 * HD), BF16),
            vmem((NX, NX, CHUNK, HD), BF16),
            vmem((NX, NX, CHUNK, 2 * HD), BF16),
            vmem((NX, NX, CHUNK, 2 * HD), F32),
            vmem((NX, NX, CHUNK, HD), F32),
            vmem((NX, NX, CHUNK, HD), BF16),
            vmem((NX, NX, 2, 1, 128), F32),
            vmem((NX, NX, CHUNK, HD), BF16),
            vmem((NX, NX, 2, 1, 128), F32),
            vmem((NX, NZ, CHUNK // NZ, HD), BF16),
            vmem((NX, NZ, CHUNK // NZ, HD), BF16),
            vmem((NZ, NX, 1, 128), I32),
            vmem((NZ * NX, 128), F32),
            vmem((HEADS, ROWS, QROWS), BF16),
            dma((4, 2)), dma((4,)), dma, dma,
            dma((TILES, 2)), dma((TILES, 2)),
            dma((6,)), dma((6,)),
            dma((NX, NX)), dma((NX, NX)), dma((NX, NX)), dma((NX, NX)),
            dma((NX, NZ)), dma((NX, NZ)),
            dma((NX,)), dma((NX,)),
            dma((NZ,)), dma((NZ,)),
        ],
        compiler_params=pltpu.CompilerParams(
            collective_id=0, has_side_effects=True, vmem_limit_bytes=56 * 1024 * 1024
        ),
    )(
        kept_index.reshape(4, 128), route.reshape(1, 128), query_pos.reshape(1, 128),
        queries, k_cache, v_cache, kept_count,
    )


def solution(mesh):
    placed = (
        P("context", "mp"),
        P("context"),
        P("context", "mp"),
        P("context", "mp"),
        P("context"),
        P("context"),
        P("context"),
    )
    return jax.shard_map(
        per_device, mesh=mesh, in_specs=placed, out_specs=P("context", "mp"), check_vma=False
    )
```
